32 devices in a mesh: tm: 4 (over y, core), height: 8 (over z, x).
Axes of the slice: x: 2, y: 2, z: 4, core: 2. Of those that a mesh axis runs over, the one named last changes fastest.
Arguments:
- queries: bfloat16 [4, 8, 2, 64, 3072], P('tm', 'height'), may hold values from -40 to 40
- keys_values: bfloat16 [4, 8, 2, 2, 64, 3072], P('tm', 'height'), may hold values from -6.2 to 6.2
- far_cubes: int32 [4, 8, 2, 24, 16], P('tm', 'height'), may hold values from 0 to 63, as said below
- out_weight: bfloat16 [3072, 3072], replicated, may hold values from -0.59765625 to 0.59765625
Outputs:
- output: bfloat16 [4, 8, 2, 64, 3072], P('tm', 'height')
The draws below stay inside these ranges and needn't reach their ends.
Inputs may be any that keep to these rules, and one draw needn't show every extreme that they name: `far_cubes`: the 16 cubes of one list are distinct. Over all cubes that one device holds, the distinct pairs (far cube, head) whose cube lies on one given device number at most 16, and exactly 16 for some given devices, from every device.
All inputs are finite; a program needn't handle non-finite values.
Results may differ from the reference program's by a relative error of at most 0.0058.
Values may be sent and summed in bfloat16 or wider, within the bound.
No kernel may reach another device: no remote copies, remote signals or barrier semaphores. Data moves between devices by JAX's collectives and lax.ppermute only.
A program may use at most 256 MiB of HBM per device.

```python
import math
import jax
import jax.numpy as jnp
from jax import lax

HEADS = 24
HEAD_DIM = 128
D = 3072
CUBE = 64
FAR = 16
SLOTS = 512
CT = 1
CH = 1
NW = 2
N_TM = 4
N_HEIGHT = 8


def attention_fields(key):
    key = jax.random.fold_in(key, 11)
    key_query, key_field = jax.random.split(key)
    grid_time = CT * N_TM
    grid_height = CH * N_HEIGHT
    width = HEADS * HEAD_DIM
    query_shape = (grid_time, grid_height, NW, CUBE, width)
    field_shape = (grid_time, grid_height, NW, 2, CUBE, width)
    queries = jnp.clip(jax.random.normal(key_query, query_shape, jnp.float32) * 2.0, -12.0, 12.0)
    fields = jnp.clip(jax.random.normal(key_field, field_shape, jnp.float32), -6.0, 6.0)
    return (queries, fields)


def draw_queries(key, part):
    return attention_fields(key)[0].astype(jnp.bfloat16)


def draw_keys_values(key, part):
    return attention_fields(key)[1].astype(jnp.bfloat16)


def draw_far_cubes(key, part):
    key = jax.random.fold_in(key, 23)
    key_order, key_cube, key_hot, key_score = jax.random.split(key, 4)
    devices = N_TM * N_HEIGHT
    capacity = SLOTS // devices
    local = CT * CH * NW
    hot_count = 4
    grid_height = CH * N_HEIGHT
    orders = jax.vmap(lambda single: jax.random.permutation(single, devices))(jax.random.split(key_order, devices))
    slot_head = (orders[:, :, None] % HEADS + jnp.arange(capacity, dtype=jnp.int32)[None, None, :]) % HEADS
    slot_head = slot_head.reshape(devices, SLOTS)
    slot_cube = jax.random.randint(key_cube, (devices, SLOTS), 0, local, dtype=jnp.int32)
    hot_owners = jax.random.permutation(key_hot, devices)[:hot_count]
    slot_owner = jnp.arange(SLOTS, dtype=jnp.int32) // capacity
    hot_slot = jnp.any(slot_owner[:, None] == hot_owners[None, :], axis=1)
    noise = jax.random.randint(key_score, (devices, local, HEADS, SLOTS), 0, 2 ** 19, dtype=jnp.int32)
    score = noise * SLOTS + jnp.arange(SLOTS, dtype=jnp.int32)[None, None, None, :]
    score = score + jnp.where(hot_slot, 2 ** 30, 0).astype(jnp.int32)[None, None, None, :]
    matching = slot_head[:, None, None, :] == jnp.arange(HEADS, dtype=jnp.int32)[None, None, :, None]
    score = jnp.where(matching, score, -1)
    picked = lax.top_k(score, FAR)[1].astype(jnp.int32)
    owner = picked // capacity
    cube_local = jnp.take_along_axis(jnp.broadcast_to(slot_cube[:, None, None, :], score.shape), picked, axis=-1)
    owner_time = owner // N_HEIGHT
    owner_height = owner % N_HEIGHT
    local_time = cube_local // (CH * NW)
    local_height = cube_local // NW % CH
    local_width = cube_local % NW
    global_time = owner_time * CT + local_time
    global_height = owner_height * CH + local_height
    numbers = (global_time * grid_height + global_height) * NW + local_width
    numbers = numbers.reshape(N_TM, N_HEIGHT, CT, CH, NW, HEADS, FAR)
    numbers = jnp.transpose(numbers, (0, 2, 1, 3, 4, 5, 6))
    return numbers.reshape(CT * N_TM, grid_height, NW, HEADS, FAR).astype(jnp.int32)


def centred(key, dims, scale, reach, held_as=jnp.bfloat16):
    result = jax.random.normal(key, dims, jnp.float32) * scale
    return jnp.minimum(jnp.maximum(result, -reach), reach).astype(held_as)


def setup_inputs(seed: int = 0) -> dict:
    splits = jax.random.split(jax.random.key(seed), 5)
    return {
        "queries": draw_queries(jax.random.fold_in(splits[4], 71), 0),
        "keys_values": draw_keys_values(jax.random.fold_in(splits[4], 71), 0),
        "far_cubes": draw_far_cubes(jax.random.fold_in(splits[4], 71), 0),
        "out_weight": centred(splits[3], (D, D), 0.1, 0.59765625),
    }


def reference(queries, keys_values, far_cubes, out_weight):
    heads = HEADS
    head_size = HEAD_DIM
    grid_time = CT * N_TM
    grid_height = CH * N_HEIGHT
    grid_width = NW
    cube_count = grid_time * grid_height * grid_width
    width = heads * head_size
    padded = jnp.pad(keys_values, ((1, 1), (1, 1), (1, 1), (0, 0), (0, 0), (0, 0)))
    flat_queries = queries.reshape(cube_count, CUBE, heads, head_size)
    flat_fields = keys_values.reshape(cube_count, 2, CUBE, heads, head_size)
    flat_far = far_cubes.reshape(cube_count, heads, FAR)
    offsets = jnp.arange(3, dtype=jnp.int32) - 1
    head_index = jnp.arange(heads, dtype=jnp.int32)
    scale = 1.0 / math.sqrt(head_size)
    zero = jnp.zeros((), jnp.int32)

    def one_cube(index):
        time_pos = (index // (grid_height * grid_width)).astype(jnp.int32)
        height_pos = (index // grid_width % grid_height).astype(jnp.int32)
        width_pos = (index % grid_width).astype(jnp.int32)
        window = lax.dynamic_slice(padded, (time_pos, height_pos, width_pos, zero, zero, zero), (3, 3, 3, 2, CUBE, width))
        window = window.reshape(27, 2, CUBE, heads, head_size)
        inside_time = (time_pos + offsets >= 0) & (time_pos + offsets < grid_time)
        inside_height = (height_pos + offsets >= 0) & (height_pos + offsets < grid_height)
        inside_width = (width_pos + offsets >= 0) & (width_pos + offsets < grid_width)
        valid = (inside_time[:, None, None] & inside_height[None, :, None] & inside_width[None, None, :]).reshape(27)
        keys_window = window[:, 0].reshape(27 * CUBE, heads, head_size).astype(jnp.float32)
        values_window = window[:, 1].reshape(27 * CUBE, heads, head_size).astype(jnp.float32)
        far_tiles = flat_fields[flat_far[index], :, :, head_index[:, None], :]
        query = flat_queries[index].astype(jnp.float32)
        score_window = jnp.einsum('qhd,khd->hqk', query, keys_window) * scale
        score_window = jnp.where(jnp.repeat(valid, CUBE)[None, None, :], score_window, -jnp.inf)
        score_far = jnp.einsum('qhd,hfkd->hqfk', query, far_tiles[:, :, 0].astype(jnp.float32)) * scale
        scores = jnp.concatenate([score_window, score_far.reshape(heads, CUBE, FAR * CUBE)], axis=-1)
        largest = lax.optimization_barrier(jnp.max(scores, axis=-1, keepdims=True))
        lifted = jnp.exp(scores - largest)
        weights = (lifted / lax.optimization_barrier(jnp.sum(lifted, axis=-1, keepdims=True))).astype(jnp.bfloat16)
        weights = lax.optimization_barrier(weights).astype(jnp.float32)
        attended = jnp.einsum('hqk,khd->qhd', weights[:, :, :27 * CUBE], values_window)
        far_weights = weights[:, :, 27 * CUBE:].reshape(heads, CUBE, FAR, CUBE)
        attended = attended + jnp.einsum('hqfk,hfkd->qhd', far_weights, far_tiles[:, :, 1].astype(jnp.float32))
        return attended.reshape(CUBE, width).astype(jnp.bfloat16)
    attended = lax.map(one_cube, jnp.arange(cube_count, dtype=jnp.int32))
    output = jnp.dot(attended.reshape(cube_count * CUBE, width), out_weight, preferred_element_type=jnp.float32)
    return output.astype(jnp.bfloat16).reshape(queries.shape)
```

```python
import functools
import math

import jax
import jax.numpy as jnp
from jax import lax
from jax.experimental import pallas as pl
from jax.experimental.pallas import tpu as pltpu
from jax.sharding import PartitionSpec as P

HEADS = 24
SLOTS = 512
HEAD_DIM = 128
LOG2E = math.log2(math.e)


def padded_2(shard, sides, width):
    for axis, dim in sides:
        peers, length = (lax.axis_size(axis), shard.shape[dim])
        up = [(i, (i + 1) % peers) for i in range(peers - 1)]
        down = [(j, i) for i, j in up]
        last = lax.slice_in_dim(shard, length - width, length, axis=dim)
        leading = lax.slice_in_dim(shard, 0, width, axis=dim)
        before = lax.ppermute(last, axis, up)
        after = lax.ppermute(leading, axis, down)
        shard = jnp.concatenate([before, shard, after], axis=dim)
    return shard


def body(queries, keys_values, far_cubes, out_weight):
    tm_count = lax.axis_size("tm")
    height_count = lax.axis_size("height")
    device_count = tm_count * height_count
    capacity = SLOTS // device_count
    span_time, span_height, span_width, cube, width = queries.shape
    heads = HEADS
    head_size = width // heads
    far_count = far_cubes.shape[-1]
    local_count = span_time * span_height * span_width
    grid_time = span_time * tm_count
    grid_height = span_height * height_count
    far_ids = far_cubes.reshape(local_count, heads, far_count)
    far_time = far_ids // (grid_height * span_width)
    far_height = far_ids // span_width % grid_height
    far_width = far_ids % span_width
    owner_dev = far_time // span_time * height_count + far_height // span_height
    local_cube = (
        far_time % span_time * span_height + far_height % span_height
    ) * span_width + far_width
    tile_code = local_cube * heads + jnp.arange(heads, dtype=jnp.int32)[None, :, None]
    wanted = (
        jnp.zeros((device_count, local_count * heads), jnp.int32).at[owner_dev, tile_code].max(1)
    )
    slot_rank = jnp.cumsum(wanted, axis=1) - 1
    far_slot = owner_dev * capacity + slot_rank[owner_dev, tile_code]
    target = jnp.where(wanted > 0, slot_rank, capacity)
    columns = jnp.broadcast_to(
        jnp.arange(local_count * heads, dtype=jnp.int32)[None, :], wanted.shape
    )
    rows = jnp.broadcast_to(jnp.arange(device_count, dtype=jnp.int32)[:, None], wanted.shape)
    requests = (
        jnp.zeros((device_count, capacity + 1), jnp.int32)
        .at[rows, target]
        .set(columns)[:, :capacity]
    )
    source = keys_values.reshape(local_count, 2, cube, heads, head_size)
    padded = padded_2(keys_values, (("tm", 0), ("height", 1)), 1)
    padded = jnp.pad(padded, ((0, 0), (0, 0), (1, 1), (0, 0), (0, 0), (0, 0)))
    asked = lax.all_to_all(requests, ("tm", "height"), split_axis=0, concat_axis=0, tiled=True)
    tiles = lax.all_to_all(
        source[asked // heads, :, :, asked % heads, :],
        ("tm", "height"),
        split_axis=0,
        concat_axis=0,
        tiled=True,
    )
    received = tiles.reshape(device_count * capacity, 2, cube, head_size)
    first_time = lax.axis_index("tm") * span_time
    first_height = lax.axis_index("height") * span_height
    offsets = jnp.arange(3, dtype=jnp.int32) - 1
    scale = 1.0 / math.sqrt(head_size)
    zero = jnp.zeros((), jnp.int32)
    flat_queries = queries.reshape(local_count, cube, heads, head_size)

    def one_cube(index):
        time_pos = index // (span_height * span_width)
        height_pos = index // span_width % span_height
        width_pos = index % span_width
        window = lax.dynamic_slice(
            padded, (time_pos, height_pos, width_pos, zero, zero, zero), (3, 3, 3, 2, cube, width)
        )
        window = window.reshape(27, 2, cube, heads, head_size)
        global_time = first_time + time_pos + offsets
        global_height = first_height + height_pos + offsets
        global_width = width_pos + offsets
        inside_time = (global_time >= 0) & (global_time < grid_time)
        inside_height = (global_height >= 0) & (global_height < grid_height)
        inside_width = (global_width >= 0) & (global_width < span_width)
        valid = (
            inside_time[:, None, None] & inside_height[None, :, None] & inside_width[None, None, :]
        ).reshape(27)
        keys_window = window[:, 0].reshape(27 * cube, heads, head_size)
        values_window = window[:, 1].reshape(27 * cube, heads, head_size)
        far_tiles = received[far_slot[index]]
        query = flat_queries[index]
        score_window = (
            jnp.einsum("qhd,khd->hqk", query, keys_window, preferred_element_type=jnp.float32)
            * scale
        )
        score_window = jnp.where(jnp.repeat(valid, cube)[None, None, :], score_window, -jnp.inf)
        score_far = (
            jnp.einsum(
                "qhd,hfkd->hqfk", query, far_tiles[:, :, 0], preferred_element_type=jnp.float32
            )
            * scale
        )
        scores = jnp.concatenate(
            [score_window, score_far.reshape(heads, cube, far_count * cube)], axis=-1
        )
        largest = jnp.max(scores, axis=-1, keepdims=True)
        lifted = jnp.exp(scores - largest)
        weights = (lifted / jnp.sum(lifted, axis=-1, keepdims=True)).astype(jnp.bfloat16)
        attended = jnp.einsum(
            "hqk,khd->qhd",
            weights[:, :, : 27 * cube],
            values_window,
            preferred_element_type=jnp.float32,
        )
        far_weights = weights[:, :, 27 * cube :].reshape(heads, cube, far_count, cube)
        attended = attended + jnp.einsum(
            "hqfk,hfkd->qhd", far_weights, far_tiles[:, :, 1], preferred_element_type=jnp.float32
        )
        return attended.reshape(cube, width).astype(jnp.bfloat16)

    attended = lax.map(one_cube, jnp.arange(local_count, dtype=jnp.int32))
    output = jnp.dot(
        attended.reshape(local_count * cube, width), out_weight, preferred_element_type=jnp.float32
    )
    return output.astype(jnp.bfloat16).reshape(queries.shape)


def prepare_kernel(q_ref, kv_ref, far_ref, small_ref, large_ref):
    groups = q_ref.shape[2] // (3 * HEAD_DIM)
    cubes = lax.broadcasted_iota(jnp.int32, (1, HEAD_DIM), 1)
    counts = jnp.zeros((far_ref.shape[0], HEAD_DIM), jnp.float32)
    for f in range(far_ref.shape[1]):
        counts += (far_ref[:, f : f + 1] == cubes).astype(jnp.float32)
    first_row = lax.broadcasted_iota(jnp.int32, (16, HEAD_DIM), 0) == 0
    heads = 3 * groups
    for chip in range(2):
        for core in range(2):
            for g in range(groups):
                to = (chip * 2 + core) * groups + g
                whole = 3 * g + 2 * chip
                shared = 3 * g + 1
                lanes = slice(whole * HEAD_DIM, (whole + 1) * HEAD_DIM)
                large_ref[to, 0:64, :] = q_ref[core, :, lanes]
                large_ref[to, 64:128, :] = kv_ref[core, 0, :, lanes]
                large_ref[to, 128:192, :] = kv_ref[core, 1, :, lanes]
                lanes = slice(shared * HEAD_DIM, (shared + 1) * HEAD_DIM)
                small_ref[to, 0:64, :] = kv_ref[core, chip, :, lanes]
                small_ref[to, 64:96, :] = q_ref[core, 32 * chip : 32 * chip + 32, lanes]
                row = core * heads
                small_ref[to, 96:112, :] = jnp.where(
                    first_row,
                    counts[row + whole : row + whole + 1],
                    counts[row + shared : row + shared + 1],
                ).astype(jnp.bfloat16)


def attend(q_at, counts_ref, keys_ref, values_ref, out_ref, bias_ref, height_count, row):
    sources, tokens = out_ref.shape[:2]
    per_block = 256 // tokens
    keys = keys_ref.shape[0]
    key_cubes = keys // 64
    chunk = 512
    listed = counts_ref[:, 96 + row, :].astype(jnp.float32)
    source = lax.broadcasted_iota(jnp.int32, listed.shape, 0)
    cube = lax.broadcasted_iota(jnp.int32, listed.shape, 1)
    other = cube // 2
    near = (jnp.abs(source // height_count - other // height_count) <= 1) & (
        jnp.abs(source % height_count - other % height_count) <= 1
    )
    counts = (listed + jnp.where(near & (cube < key_cubes), 1.0, 0.0)).astype(jnp.bfloat16)
    for start in range(0, keys, chunk):
        spread = (
            lax.broadcasted_iota(jnp.int32, (HEAD_DIM, chunk), 0)
            == (lax.broadcasted_iota(jnp.int32, (HEAD_DIM, chunk), 1) + start) // 64
        ).astype(jnp.bfloat16)
        wide = jnp.dot(counts, spread, preferred_element_type=jnp.float32)
        bias_ref[:, start : start + chunk] = jnp.where(wide < 0.5, -1e30, jnp.where(wide > 1.5, 1.0, 0.0))
    scale = LOG2E / math.sqrt(HEAD_DIM)

    def block(index, carry):
        first = index * per_block
        query = q_at(first, per_block)
        scores = []
        top = None
        for start in range(0, keys, chunk):
            raw = lax.dot_general(
                query,
                keys_ref[start : start + chunk, :],
                (((1,), (1,)), ((), ())),
                preferred_element_type=jnp.float32,
            )
            rows = [
                raw[i * tokens : (i + 1) * tokens] * scale
                + bias_ref[pl.ds(first + i, 1), start : start + chunk]
                for i in range(per_block)
            ]
            part = jnp.concatenate(rows, axis=0)
            scores.append(part)
            for lane in range(0, chunk, HEAD_DIM):
                piece = part[:, lane : lane + HEAD_DIM]
                top = piece if top is None else jnp.maximum(top, piece)
        largest = jnp.max(top, axis=1, keepdims=True)
        total = jnp.zeros((256, HEAD_DIM), jnp.float32)
        mixed = jnp.zeros((256, HEAD_DIM), jnp.float32)
        for n, start in enumerate(range(0, keys, chunk)):
            lifted = jnp.exp2(scores[n] - largest)
            for lane in range(0, chunk, HEAD_DIM):
                total += lifted[:, lane : lane + HEAD_DIM]
            mixed += jnp.dot(
                lifted.astype(jnp.bfloat16),
                values_ref[start : start + chunk, :],
                preferred_element_type=jnp.float32,
            )
        result = mixed / jnp.sum(total, axis=1, keepdims=True)
        out_ref[pl.ds(first, per_block)] = result.astype(jnp.bfloat16).reshape(
            per_block, tokens, HEAD_DIM
        )
        return carry

    lax.fori_loop(0, sources // per_block, block, 0)


def large_kernel(height_count, mine_ref, other_ref, counts_ref, out_ref, keys_ref, values_ref, bias_ref):
    core = lax.axis_index("tm") % 2
    for s in range(mine_ref.shape[0]):
        here = pl.multiple_of(s * 128 + core * 64, 64)
        there = pl.multiple_of(s * 128 + (1 - core) * 64, 64)
        keys_ref[pl.ds(here, 64), :] = mine_ref[s, 64:128, :]
        values_ref[pl.ds(here, 64), :] = mine_ref[s, 128:192, :]
        keys_ref[pl.ds(there, 64), :] = other_ref[s, 0:64, :]
        values_ref[pl.ds(there, 64), :] = other_ref[s, 64:128, :]

    def q_at(first, count):
        return mine_ref[pl.ds(first, count), 0:64, :].reshape(count * 64, HEAD_DIM)

    attend(q_at, counts_ref, keys_ref, values_ref, out_ref, bias_ref, height_count, 0)


def small_kernel(
    height_count, mine_ref, chip_ref, core_mine_ref, core_chip_ref, out_ref, keys_ref, values_ref, bias_ref
):
    core = lax.axis_index("tm") % 2
    chip = lax.axis_index("tm") // 2

    def fill(first_ref, second_ref, core_first_ref, core_second_ref):
        for s in range(mine_ref.shape[0]):
            here = pl.multiple_of(s * 128 + core * 64, 64)
            there = pl.multiple_of(s * 128 + (1 - core) * 64, 64)
            keys_ref[pl.ds(here, 64), :] = first_ref[s, 0:64, :]
            values_ref[pl.ds(here, 64), :] = second_ref[s, 0:64, :]
            keys_ref[pl.ds(there, 64), :] = core_first_ref[s]
            values_ref[pl.ds(there, 64), :] = core_second_ref[s]

    @pl.when(chip == 0)
    def _():
        fill(mine_ref, chip_ref, core_mine_ref, core_chip_ref)

    @pl.when(chip == 1)
    def _():
        fill(chip_ref, mine_ref, core_chip_ref, core_mine_ref)

    def q_at(first, count):
        return mine_ref[pl.ds(first, count), 64:96, :].reshape(count * 32, HEAD_DIM)

    attend(q_at, mine_ref, keys_ref, values_ref, out_ref, bias_ref, height_count, 1)


def by_heads(queries, keys_values, far_cubes, out_weight):
    tm_count = lax.axis_size("tm")
    height_count = lax.axis_size("height")
    devices = tm_count * height_count
    width = queries.shape[-1]
    heads = width // HEAD_DIM
    axes = ("tm", "height")
    bf16 = jnp.bfloat16
    params = pltpu.CompilerParams(vmem_limit_bytes=56 * 2**20)
    small, large = pl.pallas_call(
        prepare_kernel,
        out_shape=(
            jax.ShapeDtypeStruct((devices, 112, HEAD_DIM), bf16),
            jax.ShapeDtypeStruct((devices, 192, HEAD_DIM), bf16),
        ),
        compiler_params=params,
        name="prepare",
    )(
        queries.reshape(2, 64, width),
        keys_values.reshape(2, 2, 64, width),
        far_cubes.reshape(2 * heads, far_cubes.shape[-1]),
    )
    other_core = [(i, i ^ 1) for i in range(tm_count)]
    other_chip = [(i, i ^ 2) for i in range(tm_count)]
    scratch = [
        pltpu.VMEM((devices * 128, HEAD_DIM), bf16),
        pltpu.VMEM((devices * 128, HEAD_DIM), bf16),
        pltpu.VMEM((devices, devices * 128), jnp.float32),
    ]

    def cost(tokens):
        work = devices * tokens * devices * 128
        return pl.CostEstimate(
            flops=4 * work * HEAD_DIM, bytes_accessed=8 * 2**20, transcendentals=work
        )

    got_small = lax.all_to_all(small, axes, 0, 0, tiled=True)
    mine = got_small[:, :64]
    chip = lax.ppermute(mine, "tm", other_chip)
    core_mine = lax.ppermute(mine, "tm", other_core)
    core_chip = lax.ppermute(chip, "tm", other_core)
    out_small = pl.pallas_call(
        functools.partial(small_kernel, height_count),
        out_shape=jax.ShapeDtypeStruct((devices, 32, HEAD_DIM), bf16),
        scratch_shapes=scratch,
        compiler_params=params,
        cost_estimate=cost(32),
        name="attend_small",
    )(got_small, chip, core_mine, core_chip)

    got_large = lax.all_to_all(large, axes, 0, 0, tiled=True)
    core_large = lax.ppermute(got_large[:, 64:], "tm", other_core)
    out_large = pl.pallas_call(
        functools.partial(large_kernel, height_count),
        out_shape=jax.ShapeDtypeStruct((devices, 64, HEAD_DIM), bf16),
        scratch_shapes=scratch,
        compiler_params=params,
        cost_estimate=cost(64),
        name="attend_large",
    )(got_large, core_large, got_small)

    back_small = lax.all_to_all(out_small, axes, 0, 0, tiled=True)
    back_large = lax.all_to_all(out_large, axes, 0, 0, tiled=True)
    back_small = back_small.reshape(2, 2, height_count, 32, HEAD_DIM).transpose(1, 0, 3, 2, 4)
    back_small = back_small.reshape(2, 64, height_count, 1, HEAD_DIM)
    back_large = back_large.reshape(2, 2, height_count, 64, HEAD_DIM).transpose(1, 3, 2, 0, 4)
    attended = jnp.concatenate([back_large[:, :, :, :1], back_small, back_large[:, :, :, 1:]], axis=3)
    output = jnp.dot(
        attended.reshape(128, width), out_weight, preferred_element_type=jnp.float32
    )
    return output.astype(bf16).reshape(queries.shape)


def solution(mesh):
    in_specs = (
        P("tm", "height", None, None, None),
        P("tm", "height", None, None, None, None),
        P("tm", "height", None, None, None),
        P(),
    )
    out_specs = P("tm", "height", None, None, None)
    fits = mesh.shape["tm"] == 4 and HEADS == 3 * mesh.shape["height"]
    return jax.shard_map(by_heads if fits else body, mesh=mesh, in_specs=in_specs, out_specs=out_specs, check_vma=False)
```

```python
import functools
import math

import jax
import jax.numpy as jnp
import ml_dtypes
import numpy as np
from jax import lax
from jax.experimental import pallas as pl
from jax.experimental.pallas import tpu as pltpu
from jax.sharding import PartitionSpec as P

HEADS = 24
SLOTS = 512
HEAD_DIM = 128
LOG2E = math.log2(math.e)
SCALE = LOG2E / math.sqrt(HEAD_DIM)
TWICE = 1.0 / SCALE
TWICE_HIGH = float(np.asarray(TWICE, ml_dtypes.bfloat16))
TWICE_LOW = TWICE - TWICE_HIGH
ROWS = 256
CHUNK = 512


def padded_2(shard, sides, width):
    for axis, dim in sides:
        peers, length = (lax.axis_size(axis), shard.shape[dim])
        up = [(i, (i + 1) % peers) for i in range(peers - 1)]
        down = [(j, i) for i, j in up]
        last = lax.slice_in_dim(shard, length - width, length, axis=dim)
        leading = lax.slice_in_dim(shard, 0, width, axis=dim)
        before = lax.ppermute(last, axis, up)
        after = lax.ppermute(leading, axis, down)
        shard = jnp.concatenate([before, shard, after], axis=dim)
    return shard


def body(queries, keys_values, far_cubes, out_weight):
    tm_count = lax.axis_size("tm")
    height_count = lax.axis_size("height")
    device_count = tm_count * height_count
    capacity = SLOTS // device_count
    span_time, span_height, span_width, cube, width = queries.shape
    heads = HEADS
    head_size = width // heads
    far_count = far_cubes.shape[-1]
    local_count = span_time * span_height * span_width
    grid_time = span_time * tm_count
    grid_height = span_height * height_count
    far_ids = far_cubes.reshape(local_count, heads, far_count)
    far_time = far_ids // (grid_height * span_width)
    far_height = far_ids // span_width % grid_height
    far_width = far_ids % span_width
    owner_dev = far_time // span_time * height_count + far_height // span_height
    local_cube = (
        far_time % span_time * span_height + far_height % span_height
    ) * span_width + far_width
    tile_code = local_cube * heads + jnp.arange(heads, dtype=jnp.int32)[None, :, None]
    wanted = (
        jnp.zeros((device_count, local_count * heads), jnp.int32).at[owner_dev, tile_code].max(1)
    )
    slot_rank = jnp.cumsum(wanted, axis=1) - 1
    far_slot = owner_dev * capacity + slot_rank[owner_dev, tile_code]
    target = jnp.where(wanted > 0, slot_rank, capacity)
    columns = jnp.broadcast_to(
        jnp.arange(local_count * heads, dtype=jnp.int32)[None, :], wanted.shape
    )
    rows = jnp.broadcast_to(jnp.arange(device_count, dtype=jnp.int32)[:, None], wanted.shape)
    requests = (
        jnp.zeros((device_count, capacity + 1), jnp.int32)
        .at[rows, target]
        .set(columns)[:, :capacity]
    )
    source = keys_values.reshape(local_count, 2, cube, heads, head_size)
    padded = padded_2(keys_values, (("tm", 0), ("height", 1)), 1)
    padded = jnp.pad(padded, ((0, 0), (0, 0), (1, 1), (0, 0), (0, 0), (0, 0)))
    asked = lax.all_to_all(requests, ("tm", "height"), split_axis=0, concat_axis=0, tiled=True)
    tiles = lax.all_to_all(
        source[asked // heads, :, :, asked % heads, :],
        ("tm", "height"),
        split_axis=0,
        concat_axis=0,
        tiled=True,
    )
    received = tiles.reshape(device_count * capacity, 2, cube, head_size)
    first_time = lax.axis_index("tm") * span_time
    first_height = lax.axis_index("height") * span_height
    offsets = jnp.arange(3, dtype=jnp.int32) - 1
    scale = 1.0 / math.sqrt(head_size)
    zero = jnp.zeros((), jnp.int32)
    flat_queries = queries.reshape(local_count, cube, heads, head_size)

    def one_cube(index):
        time_pos = index // (span_height * span_width)
        height_pos = index // span_width % span_height
        width_pos = index % span_width
        window = lax.dynamic_slice(
            padded, (time_pos, height_pos, width_pos, zero, zero, zero), (3, 3, 3, 2, cube, width)
        )
        window = window.reshape(27, 2, cube, heads, head_size)
        global_time = first_time + time_pos + offsets
        global_height = first_height + height_pos + offsets
        global_width = width_pos + offsets
        inside_time = (global_time >= 0) & (global_time < grid_time)
        inside_height = (global_height >= 0) & (global_height < grid_height)
        inside_width = (global_width >= 0) & (global_width < span_width)
        valid = (
            inside_time[:, None, None] & inside_height[None, :, None] & inside_width[None, None, :]
        ).reshape(27)
        keys_window = window[:, 0].reshape(27 * cube, heads, head_size)
        values_window = window[:, 1].reshape(27 * cube, heads, head_size)
        far_tiles = received[far_slot[index]]
        query = flat_queries[index]
        score_window = (
            jnp.einsum("qhd,khd->hqk", query, keys_window, preferred_element_type=jnp.float32)
            * scale
        )
        score_window = jnp.where(jnp.repeat(valid, cube)[None, None, :], score_window, -jnp.inf)
        score_far = (
            jnp.einsum(
                "qhd,hfkd->hqfk", query, far_tiles[:, :, 0], preferred_element_type=jnp.float32
            )
            * scale
        )
        scores = jnp.concatenate(
            [score_window, score_far.reshape(heads, cube, far_count * cube)], axis=-1
        )
        largest = jnp.max(scores, axis=-1, keepdims=True)
        lifted = jnp.exp(scores - largest)
        weights = (lifted / jnp.sum(lifted, axis=-1, keepdims=True)).astype(jnp.bfloat16)
        attended = jnp.einsum(
            "hqk,khd->qhd",
            weights[:, :, : 27 * cube],
            values_window,
            preferred_element_type=jnp.float32,
        )
        far_weights = weights[:, :, 27 * cube :].reshape(heads, cube, far_count, cube)
        attended = attended + jnp.einsum(
            "hqfk,hfkd->qhd", far_weights, far_tiles[:, :, 1], preferred_element_type=jnp.float32
        )
        return attended.reshape(cube, width).astype(jnp.bfloat16)

    attended = lax.map(one_cube, jnp.arange(local_count, dtype=jnp.int32))
    output = jnp.dot(
        attended.reshape(local_count * cube, width), out_weight, preferred_element_type=jnp.float32
    )
    return output.astype(jnp.bfloat16).reshape(queries.shape)


def head_lanes(head):
    return slice(head * HEAD_DIM, (head + 1) * HEAD_DIM)


def prepare_first(q_ref, kv_ref, far_ref, out_ref, q_in, kv_in, staged, sems):
    groups = out_ref.shape[2]
    span = 3 * HEAD_DIM

    def copies_in(g):
        lanes = pl.ds(g * span, span)
        return (
            pltpu.make_async_copy(q_ref.at[:, :, lanes], q_in.at[g], sems.at[0, g]),
            pltpu.make_async_copy(kv_ref.at[:, :, :, lanes], kv_in.at[g], sems.at[1, g]),
        )

    def copy_out(g):
        return pltpu.make_async_copy(staged.at[:, :, g], out_ref.at[:, :, g], sems.at[2, g])

    for g in range(groups):
        for copy in copies_in(g):
            copy.start()
    cubes = lax.broadcasted_iota(jnp.int32, (far_ref.shape[1], HEAD_DIM), 1) % 64
    top_row = lax.broadcasted_iota(jnp.int32, (8, HEAD_DIM), 0) == 0

    def counts(core, head):
        listed = far_ref[core, :, head : head + 1] == cubes
        return jnp.sum(listed.astype(jnp.float32), axis=0, keepdims=True)

    for g in range(groups):
        for core in range(2):
            shared = counts(core, 3 * g + 1)
            for chip in range(2):
                staged[chip, core, g, 256:264, :] = jnp.where(
                    top_row, counts(core, 3 * g + 2 * chip), shared
                ).astype(jnp.bfloat16)
    for g in range(groups):
        for copy in copies_in(g):
            copy.wait()
        for core in range(2):
            for chip in range(2):
                lanes = head_lanes(2 * chip)
                staged[chip, core, g, 0:64, :] = q_in[g, core, :, lanes]
                staged[chip, core, g, 64:128, :] = kv_in[g, core, 0, :, lanes]
                staged[chip, core, g, 128:192, :] = kv_in[g, core, 1, :, lanes]
                staged[chip, core, g, 192:256, :] = kv_in[g, core, chip, :, head_lanes(1)]
        copy_out(g).start()
    for g in range(groups):
        copy_out(g).wait()


def prepare_second(q_ref, out_ref, sems):
    copies = []
    for g in range(out_ref.shape[2]):
        lanes = pl.ds((3 * g + 1) * HEAD_DIM, HEAD_DIM)
        for chip in range(2):
            copies.append(
                pltpu.make_async_copy(
                    q_ref.at[:, 32 * chip : 32 * chip + 32, lanes],
                    out_ref.at[chip, :, g],
                    sems.at[chip, g],
                )
            )
    for copy in copies:
        copy.start()
    for copy in copies:
        copy.wait()


def set_constants(listed, bias_ref, height_count):
    source = lax.broadcasted_iota(jnp.int32, listed.shape, 0)
    lane = lax.broadcasted_iota(jnp.int32, listed.shape, 1)
    place = lane % 64 // 2
    near = (jnp.abs(source // height_count - place // height_count) <= 1) & (
        jnp.abs(source % height_count - place % height_count) <= 1
    )
    counts = listed + jnp.where(near, 1.0, 0.0)
    high = lane < 64
    bias_ref[...] = jnp.where(
        counts < 0.5,
        jnp.where(high, -1e30, 0.0),
        jnp.where(counts > 1.5, jnp.where(high, TWICE_HIGH, TWICE_LOW), 0.0),
    )


def set_margins(kv_ref):
    shape = (2, 64, HEAD_DIM)
    width = lax.broadcasted_iota(jnp.int32, shape, 0)
    lane = lax.broadcasted_iota(jnp.int32, shape, 2) % 64
    for s in range(kv_ref.shape[1]):
        kv_ref[0, s, :, :, HEAD_DIM:] = (lane == 2 * s + width).astype(jnp.bfloat16)
        kv_ref[1, s, :, :, HEAD_DIM:] = jnp.ones(shape, jnp.bfloat16)


def attend(q_at, wait_values, kv_ref, bias_ref, out_ref, scores):
    sources, tokens = out_ref.shape[:2]
    step = ROWS // tokens
    chunk = CHUNK // 128
    chunks = range(0, sources, chunk)

    def score(first, s_ref):
        bias = [
            jnp.broadcast_to(bias_ref[pl.ds(first + i, 1), :], (tokens, HEAD_DIM))
            for i in range(step)
        ]
        bias = jnp.concatenate(bias, axis=0).astype(jnp.bfloat16)
        query = jnp.concatenate([q_at(first, step), bias], axis=1)
        top = None
        for s in chunks:
            part = lax.dot_general(
                query,
                kv_ref[0, s : s + chunk].reshape(CHUNK, 2 * HEAD_DIM),
                (((1,), (1,)), ((), ())),
                preferred_element_type=jnp.float32,
            )
            s_ref[:, s * 128 : s * 128 + CHUNK] = part
            for lane in range(0, CHUNK, HEAD_DIM):
                piece = part[:, lane : lane + HEAD_DIM]
                top = piece if top is None else jnp.maximum(top, piece)
        return jnp.max(top, axis=1, keepdims=True)

    def mix(first, s_ref, largest):
        mixed = jnp.zeros((ROWS, 2 * HEAD_DIM), jnp.float32)
        for s in chunks:
            lifted = jnp.exp2((s_ref[:, s * 128 : s * 128 + CHUNK] - largest) * SCALE)
            mixed += jnp.dot(
                lifted.astype(jnp.bfloat16),
                kv_ref[1, s : s + chunk].reshape(CHUNK, 2 * HEAD_DIM),
                preferred_element_type=jnp.float32,
            )
        result = (mixed[:, :HEAD_DIM] / mixed[:, HEAD_DIM:]).astype(out_ref.dtype)
        out_ref[pl.ds(first, step)] = result.reshape(step, tokens, HEAD_DIM)

    def two_blocks(index, largest):
        first = index * 2 * step
        later = score(first + step, scores[1])
        mix(first, scores[0], largest)
        following = jnp.minimum(first + 2 * step, sources - step)
        largest = score(following, scores[0])
        mix(first + step, scores[1], later)
        return largest

    largest = score(0, scores[0])
    wait_values()
    lax.fori_loop(0, sources // step // 2, two_blocks, largest)


def pieces(count, source, target, sems, row):
    part = count // 4
    return [
        pltpu.make_async_copy(
            source(pl.ds(i * part, part)), target(pl.ds(i * part, part)), sems.at[row, i]
        )
        for i in range(4)
    ]


def large_kernel(
    height_count, mine_ref, core_ref, info_in, out_ref, kv_ref, q_in, bias_ref, sems, *scores
):
    core = lax.axis_index("tm") % 2
    count = mine_ref.shape[0]
    own = [
        pieces(
            count,
            lambda at, k=k: mine_ref.at[at, 64 + 64 * k : 128 + 64 * k, :],
            lambda at, k=k: kv_ref.at[k, at, core, :, 0:HEAD_DIM],
            sems,
            k,
        )
        for k in range(2)
    ]
    other = [
        pieces(
            count,
            lambda at, k=k: core_ref.at[at, 64 * k : 64 + 64 * k, :],
            lambda at, k=k: kv_ref.at[k, at, 1 - core, :, 0:HEAD_DIM],
            sems,
            2 + k,
        )
        for k in range(2)
    ]
    query = pieces(count, lambda at: mine_ref.at[at, 0:64, :], lambda at: q_in.at[at], sems, 4)
    for copy in own[0] + other[0] + query + own[1] + other[1]:
        copy.start()
    set_margins(kv_ref)
    set_constants(info_in[:, 0, :].astype(jnp.float32), bias_ref, height_count)
    for copy in own[0] + other[0] + query:
        copy.wait()

    def wait_values():
        for copy in own[1] + other[1]:
            copy.wait()

    def q_at(first, count):
        return q_in[pl.ds(first, count)].reshape(count * 64, HEAD_DIM)

    attend(q_at, wait_values, kv_ref, bias_ref, out_ref, scores)


def small_kernel(
    height_count, first_ref, second_ref, chip_ref, core_mine_ref, core_chip_ref, info_in, out_ref,
    kv_ref, q_in, bias_ref, sems, *scores
):
    core = lax.axis_index("tm") % 2
    chip = lax.axis_index("tm") // 2
    count = first_ref.shape[0]

    def kept(source, kind, width, row):
        return pieces(
            count, source, lambda at: kv_ref.at[kind, at, width, :, 0:HEAD_DIM], sems, row
        )

    copies = pieces(count, lambda at: second_ref.at[at], lambda at: q_in.at[at], sems, 4)
    copies += kept(lambda at: first_ref.at[at, 192:256, :], chip, core, 0)
    copies += kept(lambda at: chip_ref.at[at], 1 - chip, core, 1)
    copies += kept(lambda at: core_mine_ref.at[at], chip, 1 - core, 2)
    copies += kept(lambda at: core_chip_ref.at[at], 1 - chip, 1 - core, 3)
    for copy in copies:
        copy.start()
    set_margins(kv_ref)
    set_constants(info_in[:, 1, :].astype(jnp.float32), bias_ref, height_count)
    for copy in copies:
        copy.wait()

    def q_at(first, count):
        return q_in[pl.ds(first, count)].reshape(count * 32, HEAD_DIM)

    attend(q_at, lambda: None, kv_ref, bias_ref, out_ref, scores)


def project_large(back_ref, weight_ref, part_ref, rest_ref, weights, sems):
    groups = back_ref.shape[0] // 4

    def copies(g):
        return [
            pltpu.make_async_copy(weight_ref.at[g, 2 * chip], weights.at[chip, g], sems.at[chip, g])
            for chip in range(2)
        ]

    def rest(g):
        return pltpu.make_async_copy(weight_ref.at[g, 1], rest_ref.at[g], sems.at[2, g])

    for g in range(groups):
        for copy in copies(g):
            copy.start()
    for g in range(groups):
        rest(g).start()
    total = None
    for g in range(0, groups, 2):
        for copy in copies(g) + copies(g + 1):
            copy.wait()
        for chip in range(2):
            rows = [
                jnp.concatenate(
                    [back_ref[(chip * 2 + core) * groups + g + i] for i in range(2)], axis=1
                )
                for core in range(2)
            ]
            part = jnp.dot(
                jnp.concatenate(rows, axis=0),
                weights[chip, g : g + 2].reshape(2 * HEAD_DIM, weights.shape[-1]),
                preferred_element_type=jnp.float32,
            )
            total = part if total is None else total + part
    part_ref[...] = total
    for g in range(groups):
        rest(g).wait()


def project_small(back_ref, weight_ref, part_ref, out_ref):
    groups = back_ref.shape[0] // 4
    rows = [
        jnp.concatenate([back_ref[to * groups + g] for g in range(groups)], axis=1)
        for to in (0, 2, 1, 3)
    ]
    attended = jnp.concatenate(rows, axis=0)
    width = out_ref.shape[-1]
    tile = width // 4
    for start in range(0, width, tile):
        weight = weight_ref[:, :, start : start + tile].reshape(groups * HEAD_DIM, tile)
        total = part_ref[:, start : start + tile] + jnp.dot(
            attended, weight, preferred_element_type=jnp.float32
        )
        out_ref[:, start : start + tile] = total.astype(out_ref.dtype)


def by_heads(queries, keys_values, far_cubes, out_weight):
    tm_count = lax.axis_size("tm")
    height_count = lax.axis_size("height")
    devices = tm_count * height_count
    width = queries.shape[-1]
    heads = width // HEAD_DIM
    far_count = far_cubes.shape[-1]
    axes = ("tm", "height")
    bf16, f32 = jnp.bfloat16, jnp.float32
    params = pltpu.CompilerParams(vmem_limit_bytes=60 * 2**20)
    anywhere = pl.BlockSpec(memory_space=pl.ANY)
    queries_in = queries.reshape(2, 64, width)
    fields_in = keys_values.reshape(2, 2, 64, width)

    first = pl.pallas_call(
        prepare_first,
        in_specs=[anywhere, anywhere, pl.BlockSpec(memory_space=pltpu.VMEM)],
        out_specs=anywhere,
        out_shape=jax.ShapeDtypeStruct((2, 2, height_count, 264, HEAD_DIM), bf16),
        scratch_shapes=[
            pltpu.VMEM((height_count, 2, 64, 3 * HEAD_DIM), bf16),
            pltpu.VMEM((height_count, 2, 2, 64, 3 * HEAD_DIM), bf16),
            pltpu.VMEM((2, 2, height_count, 264, HEAD_DIM), bf16),
            pltpu.SemaphoreType.DMA((3, height_count)),
        ],
        compiler_params=params,
        name="prepare_first",
    )(queries_in, fields_in, far_cubes.reshape(2, heads, far_count).transpose(0, 2, 1))
    second = pl.pallas_call(
        prepare_second,
        in_specs=[anywhere],
        out_specs=anywhere,
        out_shape=jax.ShapeDtypeStruct((2, 2, height_count, 32, HEAD_DIM), bf16),
        scratch_shapes=[pltpu.SemaphoreType.DMA((2, height_count))],
        compiler_params=params,
        cost_estimate=pl.CostEstimate(flops=0, bytes_accessed=2**20, transcendentals=0),
        name="prepare_second",
    )(queries_in)

    def exchange(x):
        return lax.all_to_all(x, axes, 0, 0, tiled=True)

    def swap(x, distance):
        return lax.ppermute(x, "tm", [(i, i ^ distance) for i in range(tm_count)])

    def attention(kernel, name, tokens, specs):
        keys = devices * 128
        work = devices * tokens * keys
        return pl.pallas_call(
            functools.partial(kernel, height_count),
            in_specs=specs,
            out_shape=jax.ShapeDtypeStruct((devices, tokens, HEAD_DIM), bf16),
            scratch_shapes=[
                pltpu.VMEM((2, devices, 2, 64, 2 * HEAD_DIM), bf16),
                pltpu.VMEM((devices, tokens, HEAD_DIM), bf16),
                pltpu.VMEM((devices, HEAD_DIM), f32),
                pltpu.SemaphoreType.DMA((5, 4)),
                pltpu.VMEM((ROWS, keys), f32),
                pltpu.VMEM((ROWS, keys), f32),
            ],
            compiler_params=params,
            cost_estimate=pl.CostEstimate(
                flops=8 * work * HEAD_DIM, bytes_accessed=4 * 2**20, transcendentals=work
            ),
            name=name,
        )

    vmem = pl.BlockSpec(memory_space=pltpu.VMEM)
    got_first = exchange(first.reshape(devices, 264, HEAD_DIM))
    large = got_first[:, 64:192]
    small = got_first[:, 192:256]
    info = got_first[:, 256:264]
    second, large = lax.optimization_barrier((second, large))
    got_second = exchange(second.reshape(devices, 32, HEAD_DIM))
    core_large = swap(large, 1)
    chip = swap(small, 2)
    core_small = swap(small, 1)
    out_large = attention(large_kernel, "attend_large", 64, [anywhere, anywhere, vmem])(
        got_first, core_large, info
    )
    core_chip = swap(chip, 1)

    got_second, out_large = lax.optimization_barrier((got_second, out_large))
    back_large = exchange(out_large)
    out_small = attention(small_kernel, "attend_small", 32, [anywhere] * 5 + [vmem])(
        got_first, got_second, chip, core_small, core_chip, info
    )
    back_large, out_small = lax.optimization_barrier((back_large, out_small))
    back_small = exchange(out_small)
    by_head = out_weight.reshape(height_count, 3, HEAD_DIM, width)
    part, rest = pl.pallas_call(
        project_large,
        in_specs=[vmem, anywhere],
        out_specs=(vmem, vmem),
        out_shape=(
            pltpu.VMEM((128, width), f32),
            pltpu.VMEM((height_count, HEAD_DIM, width), bf16),
        ),
        scratch_shapes=[
            pltpu.VMEM((2, height_count, HEAD_DIM, width), bf16),
            pltpu.SemaphoreType.DMA((3, height_count)),
        ],
        compiler_params=pltpu.CompilerParams(vmem_limit_bytes=40 * 2**20),
        cost_estimate=pl.CostEstimate(
            flops=4 * 128 * width * width // 3, bytes_accessed=20 * 2**20, transcendentals=0
        ),
        name="project_large",
    )(back_large, by_head)
    back_small, part = lax.optimization_barrier((back_small, part))
    output = pl.pallas_call(
        project_small,
        in_specs=[vmem, vmem, vmem],
        out_shape=jax.ShapeDtypeStruct((128, width), bf16),
        compiler_params=pltpu.CompilerParams(vmem_limit_bytes=40 * 2**20),
        cost_estimate=pl.CostEstimate(
            flops=2 * 128 * width * width // 3, bytes_accessed=8 * 2**20, transcendentals=0
        ),
        name="project_small",
    )(back_small, rest, part)
    return output.reshape(queries.shape)


def solution(mesh):
    in_specs = (
        P("tm", "height", None, None, None),
        P("tm", "height", None, None, None, None),
        P("tm", "height", None, None, None),
        P(),
    )
    out_specs = P("tm", "height", None, None, None)
    fits = mesh.shape["tm"] == 4 and HEADS == 3 * mesh.shape["height"]
    return jax.shard_map(by_heads if fits else body, mesh=mesh, in_specs=in_specs, out_specs=out_specs, check_vma=False)
```

```python
import functools
import math

import jax
import jax.numpy as jnp
import ml_dtypes
import numpy as np
from jax import lax
from jax.experimental import pallas as pl
from jax.experimental.pallas import tpu as pltpu
from jax.sharding import PartitionSpec as P

HEADS = 24
SLOTS = 512
HEAD_DIM = 128
LOG2E = math.log2(math.e)
SCALE = LOG2E / math.sqrt(HEAD_DIM)
TWICE = 1.0 / SCALE
TWICE_HIGH = float(np.asarray(TWICE, ml_dtypes.bfloat16))
TWICE_LOW = TWICE - TWICE_HIGH
ROWS = 256
CHUNK = 512


def padded_2(shard, sides, width):
    for axis, dim in sides:
        peers, length = (lax.axis_size(axis), shard.shape[dim])
        up = [(i, (i + 1) % peers) for i in range(peers - 1)]
        down = [(j, i) for i, j in up]
        last = lax.slice_in_dim(shard, length - width, length, axis=dim)
        leading = lax.slice_in_dim(shard, 0, width, axis=dim)
        before = lax.ppermute(last, axis, up)
        after = lax.ppermute(leading, axis, down)
        shard = jnp.concatenate([before, shard, after], axis=dim)
    return shard


def body(queries, keys_values, far_cubes, out_weight):
    tm_count = lax.axis_size("tm")
    height_count = lax.axis_size("height")
    device_count = tm_count * height_count
    capacity = SLOTS // device_count
    span_time, span_height, span_width, cube, width = queries.shape
    heads = HEADS
    head_size = width // heads
    far_count = far_cubes.shape[-1]
    local_count = span_time * span_height * span_width
    grid_time = span_time * tm_count
    grid_height = span_height * height_count
    far_ids = far_cubes.reshape(local_count, heads, far_count)
    far_time = far_ids // (grid_height * span_width)
    far_height = far_ids // span_width % grid_height
    far_width = far_ids % span_width
    owner_dev = far_time // span_time * height_count + far_height // span_height
    local_cube = (
        far_time % span_time * span_height + far_height % span_height
    ) * span_width + far_width
    tile_code = local_cube * heads + jnp.arange(heads, dtype=jnp.int32)[None, :, None]
    wanted = (
        jnp.zeros((device_count, local_count * heads), jnp.int32).at[owner_dev, tile_code].max(1)
    )
    slot_rank = jnp.cumsum(wanted, axis=1) - 1
    far_slot = owner_dev * capacity + slot_rank[owner_dev, tile_code]
    target = jnp.where(wanted > 0, slot_rank, capacity)
    columns = jnp.broadcast_to(
        jnp.arange(local_count * heads, dtype=jnp.int32)[None, :], wanted.shape
    )
    rows = jnp.broadcast_to(jnp.arange(device_count, dtype=jnp.int32)[:, None], wanted.shape)
    requests = (
        jnp.zeros((device_count, capacity + 1), jnp.int32)
        .at[rows, target]
        .set(columns)[:, :capacity]
    )
    source = keys_values.reshape(local_count, 2, cube, heads, head_size)
    padded = padded_2(keys_values, (("tm", 0), ("height", 1)), 1)
    padded = jnp.pad(padded, ((0, 0), (0, 0), (1, 1), (0, 0), (0, 0), (0, 0)))
    asked = lax.all_to_all(requests, ("tm", "height"), split_axis=0, concat_axis=0, tiled=True)
    tiles = lax.all_to_all(
        source[asked // heads, :, :, asked % heads, :],
        ("tm", "height"),
        split_axis=0,
        concat_axis=0,
        tiled=True,
    )
    received = tiles.reshape(device_count * capacity, 2, cube, head_size)
    first_time = lax.axis_index("tm") * span_time
    first_height = lax.axis_index("height") * span_height
    offsets = jnp.arange(3, dtype=jnp.int32) - 1
    scale = 1.0 / math.sqrt(head_size)
    zero = jnp.zeros((), jnp.int32)
    flat_queries = queries.reshape(local_count, cube, heads, head_size)

    def one_cube(index):
        time_pos = index // (span_height * span_width)
        height_pos = index // span_width % span_height
        width_pos = index % span_width
        window = lax.dynamic_slice(
            padded, (time_pos, height_pos, width_pos, zero, zero, zero), (3, 3, 3, 2, cube, width)
        )
        window = window.reshape(27, 2, cube, heads, head_size)
        global_time = first_time + time_pos + offsets
        global_height = first_height + height_pos + offsets
        global_width = width_pos + offsets
        inside_time = (global_time >= 0) & (global_time < grid_time)
        inside_height = (global_height >= 0) & (global_height < grid_height)
        inside_width = (global_width >= 0) & (global_width < span_width)
        valid = (
            inside_time[:, None, None] & inside_height[None, :, None] & inside_width[None, None, :]
        ).reshape(27)
        keys_window = window[:, 0].reshape(27 * cube, heads, head_size)
        values_window = window[:, 1].reshape(27 * cube, heads, head_size)
        far_tiles = received[far_slot[index]]
        query = flat_queries[index]
        score_window = (
            jnp.einsum("qhd,khd->hqk", query, keys_window, preferred_element_type=jnp.float32)
            * scale
        )
        score_window = jnp.where(jnp.repeat(valid, cube)[None, None, :], score_window, -jnp.inf)
        score_far = (
            jnp.einsum(
                "qhd,hfkd->hqfk", query, far_tiles[:, :, 0], preferred_element_type=jnp.float32
            )
            * scale
        )
        scores = jnp.concatenate(
            [score_window, score_far.reshape(heads, cube, far_count * cube)], axis=-1
        )
        largest = jnp.max(scores, axis=-1, keepdims=True)
        lifted = jnp.exp(scores - largest)
        weights = (lifted / jnp.sum(lifted, axis=-1, keepdims=True)).astype(jnp.bfloat16)
        attended = jnp.einsum(
            "hqk,khd->qhd",
            weights[:, :, : 27 * cube],
            values_window,
            preferred_element_type=jnp.float32,
        )
        far_weights = weights[:, :, 27 * cube :].reshape(heads, cube, far_count, cube)
        attended = attended + jnp.einsum(
            "hqfk,hfkd->qhd", far_weights, far_tiles[:, :, 1], preferred_element_type=jnp.float32
        )
        return attended.reshape(cube, width).astype(jnp.bfloat16)

    attended = lax.map(one_cube, jnp.arange(local_count, dtype=jnp.int32))
    output = jnp.dot(
        attended.reshape(local_count * cube, width), out_weight, preferred_element_type=jnp.float32
    )
    return output.astype(jnp.bfloat16).reshape(queries.shape)


def head_lanes(head):
    return slice(head * HEAD_DIM, (head + 1) * HEAD_DIM)


def prepare_first(q_ref, kv_ref, far_ref, out_ref, q_in, kv_in, staged, sems):
    groups = out_ref.shape[2]
    span = 3 * HEAD_DIM

    def copies_in(g):
        lanes = pl.ds(g * span, span)
        return (
            pltpu.make_async_copy(q_ref.at[:, :, lanes], q_in.at[g], sems.at[0, g]),
            pltpu.make_async_copy(kv_ref.at[:, :, :, lanes], kv_in.at[g], sems.at[1, g]),
        )

    def copy_out(g):
        return pltpu.make_async_copy(staged.at[:, :, g], out_ref.at[:, :, g], sems.at[2, g])

    for g in range(groups):
        for copy in copies_in(g):
            copy.start()
    cubes = lax.broadcasted_iota(jnp.int32, (far_ref.shape[1], HEAD_DIM), 1) % 64
    top_row = lax.broadcasted_iota(jnp.int32, (8, HEAD_DIM), 0) == 0

    def counts(core, head):
        listed = far_ref[core, :, head : head + 1] == cubes
        return jnp.sum(listed.astype(jnp.float32), axis=0, keepdims=True)

    for g in range(groups):
        for core in range(2):
            shared = counts(core, 3 * g + 1)
            for chip in range(2):
                staged[chip, core, g, 256:264, :] = jnp.where(
                    top_row, counts(core, 3 * g + 2 * chip), shared
                ).astype(jnp.bfloat16)
    for g in range(groups):
        for copy in copies_in(g):
            copy.wait()
        for core in range(2):
            for chip in range(2):
                lanes = head_lanes(2 * chip)
                staged[chip, core, g, 0:64, :] = q_in[g, core, :, lanes]
                staged[chip, core, g, 64:128, :] = kv_in[g, core, 0, :, lanes]
                staged[chip, core, g, 128:192, :] = kv_in[g, core, 1, :, lanes]
                staged[chip, core, g, 192:256, :] = kv_in[g, core, chip, :, head_lanes(1)]
        copy_out(g).start()
    for g in range(groups):
        copy_out(g).wait()


def prepare_second(q_ref, out_ref, sems):
    copies = []
    for g in range(out_ref.shape[2]):
        lanes = pl.ds((3 * g + 1) * HEAD_DIM, HEAD_DIM)
        for chip in range(2):
            copies.append(
                pltpu.make_async_copy(
                    q_ref.at[:, 32 * chip : 32 * chip + 32, lanes],
                    out_ref.at[chip, :, g],
                    sems.at[chip, g],
                )
            )
    for copy in copies:
        copy.start()
    for copy in copies:
        copy.wait()


def set_constants(listed, bias_ref, height_count):
    source = lax.broadcasted_iota(jnp.int32, listed.shape, 0)
    lane = lax.broadcasted_iota(jnp.int32, listed.shape, 1)
    place = lane % 64 // 2
    near = (jnp.abs(source // height_count - place // height_count) <= 1) & (
        jnp.abs(source % height_count - place % height_count) <= 1
    )
    counts = listed + jnp.where(near, 1.0, 0.0)
    high = lane < 64
    bias_ref[...] = jnp.where(
        counts < 0.5,
        jnp.where(high, -1e30, 0.0),
        jnp.where(counts > 1.5, jnp.where(high, TWICE_HIGH, TWICE_LOW), 0.0),
    )


def set_margins(kv_ref):
    shape = (2, 64, HEAD_DIM)
    width = lax.broadcasted_iota(jnp.int32, shape, 0)
    lane = lax.broadcasted_iota(jnp.int32, shape, 2) % 64
    for s in range(kv_ref.shape[1]):
        kv_ref[0, s, :, :, HEAD_DIM:] = (lane == 2 * s + width).astype(jnp.bfloat16)
        kv_ref[1, s, :, :, HEAD_DIM:] = jnp.ones(shape, jnp.bfloat16)


def attend(q_at, wait_values, kv_ref, bias_ref, out_ref, scores):
    sources, tokens = out_ref.shape[:2]
    step = ROWS // tokens
    chunk = CHUNK // 128
    chunks = range(0, sources, chunk)

    def score(first, s_ref):
        bias = [
            jnp.broadcast_to(bias_ref[pl.ds(first + i, 1), :], (tokens, HEAD_DIM))
            for i in range(step)
        ]
        bias = jnp.concatenate(bias, axis=0).astype(jnp.bfloat16)
        query = jnp.concatenate([q_at(first, step), bias], axis=1)
        top = None
        for s in chunks:
            part = lax.dot_general(
                query,
                kv_ref[0, s : s + chunk].reshape(CHUNK, 2 * HEAD_DIM),
                (((1,), (1,)), ((), ())),
                preferred_element_type=jnp.float32,
            )
            s_ref[:, s * 128 : s * 128 + CHUNK] = part
            for lane in range(0, CHUNK, HEAD_DIM):
                piece = part[:, lane : lane + HEAD_DIM]
                top = piece if top is None else jnp.maximum(top, piece)
        return jnp.max(top, axis=1, keepdims=True)

    def mix(first, s_ref, largest):
        mixed = jnp.zeros((ROWS, 2 * HEAD_DIM), jnp.float32)
        for s in chunks:
            lifted = jnp.exp2((s_ref[:, s * 128 : s * 128 + CHUNK] - largest) * SCALE)
            mixed += jnp.dot(
                lifted.astype(jnp.bfloat16),
                kv_ref[1, s : s + chunk].reshape(CHUNK, 2 * HEAD_DIM),
                preferred_element_type=jnp.float32,
            )
        result = (mixed[:, :HEAD_DIM] / mixed[:, HEAD_DIM:]).astype(out_ref.dtype)
        out_ref[pl.ds(first, step)] = result.reshape(step, tokens, HEAD_DIM)

    def two_blocks(index, largest):
        first = index * 2 * step
        later = score(first + step, scores[1])
        mix(first, scores[0], largest)
        largest = score(first + 2 * step, scores[0])
        mix(first + step, scores[1], later)
        return largest

    largest = score(0, scores[0])
    wait_values()
    largest = lax.fori_loop(0, sources // step // 2 - 1, two_blocks, largest)
    last = sources - step
    later = score(last, scores[1])
    mix(last - step, scores[0], largest)
    mix(last, scores[1], later)


def pieces(count, source, target, sems, row):
    part = count // 4
    return [
        pltpu.make_async_copy(
            source(pl.ds(i * part, part)), target(pl.ds(i * part, part)), sems.at[row, i]
        )
        for i in range(4)
    ]


def large_kernel(
    height_count, mine_ref, core_ref, info_in, out_ref, kv_ref, q_in, bias_ref, sems, *scores
):
    core = lax.axis_index("tm") % 2
    count = mine_ref.shape[0]
    own = [
        pieces(
            count,
            lambda at, k=k: mine_ref.at[at, 64 + 64 * k : 128 + 64 * k, :],
            lambda at, k=k: kv_ref.at[k, at, core, :, 0:HEAD_DIM],
            sems,
            k,
        )
        for k in range(2)
    ]
    other = [
        pieces(
            count,
            lambda at, k=k: core_ref.at[at, 64 + 64 * k : 128 + 64 * k, :],
            lambda at, k=k: kv_ref.at[k, at, 1 - core, :, 0:HEAD_DIM],
            sems,
            2 + k,
        )
        for k in range(2)
    ]
    query = pieces(count, lambda at: mine_ref.at[at, 0:64, :], lambda at: q_in.at[at], sems, 4)
    for copy in own[0] + other[0] + query + own[1] + other[1]:
        copy.start()
    set_margins(kv_ref)
    set_constants(info_in[:, 0, :].astype(jnp.float32), bias_ref, height_count)
    for copy in own[0] + other[0] + query:
        copy.wait()

    def wait_values():
        for copy in own[1] + other[1]:
            copy.wait()

    def q_at(first, count):
        return q_in[pl.ds(first, count)].reshape(count * 64, HEAD_DIM)

    attend(q_at, wait_values, kv_ref, bias_ref, out_ref, scores)


def small_kernel(
    height_count, first_ref, second_ref, chip_ref, core_first_ref, core_chip_ref, info_in, out_ref,
    kv_ref, q_in, bias_ref, sems, *scores
):
    core = lax.axis_index("tm") % 2
    chip = lax.axis_index("tm") // 2
    count = first_ref.shape[0]

    def kept(source, kind, width, row):
        return pieces(
            count, source, lambda at: kv_ref.at[kind, at, width, :, 0:HEAD_DIM], sems, row
        )

    copies = pieces(count, lambda at: second_ref.at[at], lambda at: q_in.at[at], sems, 4)
    copies += kept(lambda at: first_ref.at[at, 192:256, :], chip, core, 0)
    copies += kept(lambda at: chip_ref.at[at], 1 - chip, core, 1)
    copies += kept(lambda at: core_first_ref.at[at, 192:256, :], chip, 1 - core, 2)
    copies += kept(lambda at: core_chip_ref.at[at], 1 - chip, 1 - core, 3)
    for copy in copies:
        copy.start()
    set_margins(kv_ref)
    set_constants(info_in[:, 1, :].astype(jnp.float32), bias_ref, height_count)
    for copy in copies:
        copy.wait()

    def q_at(first, count):
        return q_in[pl.ds(first, count)].reshape(count * 32, HEAD_DIM)

    attend(q_at, lambda: None, kv_ref, bias_ref, out_ref, scores)


def side_by_side(refs, rows):
    return jnp.concatenate([jnp.concatenate([refs[i] for i in row], axis=1) for row in rows], axis=0)


def project_large(back_ref, weight_ref, part_ref, weights, sems):
    groups = back_ref.shape[0] // 4

    def copies(g):
        return [
            pltpu.make_async_copy(weight_ref.at[g, 2 * chip], weights.at[chip, g], sems.at[chip, g])
            for chip in range(2)
        ]

    for g in range(groups):
        for copy in copies(g):
            copy.start()
    total = None
    for g in range(0, groups, 2):
        for copy in copies(g) + copies(g + 1):
            copy.wait()
        for chip in range(2):
            first = chip * 2 * groups + g
            rows = [[first + core * groups + i for i in range(2)] for core in range(2)]
            part = jnp.dot(
                side_by_side(back_ref, rows),
                weights[chip, g : g + 2].reshape(2 * HEAD_DIM, weights.shape[-1]),
                preferred_element_type=jnp.float32,
            )
            total = part if total is None else total + part
    part_ref[...] = total


def project_small(back_ref, weight_ref, part_ref, out_ref, weights, sems):
    groups = back_ref.shape[0] // 4
    tiles = sems.shape[0]
    tile = weights.shape[-1]

    def copies(n):
        return [
            pltpu.make_async_copy(
                weight_ref.at[g, 1, :, n * tile : (n + 1) * tile], weights.at[n, g], sems.at[n, g]
            )
            for g in range(groups)
        ]

    for n in range(tiles):
        for copy in copies(n):
            copy.start()
    rows = [[to * groups + g for g in range(groups)] for to in (0, 2, 1, 3)]
    attended = side_by_side(back_ref, rows)
    for n in range(tiles):
        for copy in copies(n):
            copy.wait()
        lanes = slice(n * tile, (n + 1) * tile)
        total = part_ref[:, lanes] + jnp.dot(
            attended,
            weights[n].reshape(groups * HEAD_DIM, tile),
            preferred_element_type=jnp.float32,
        )
        out_ref[:, lanes] = total.astype(out_ref.dtype)


def by_heads(queries, keys_values, far_cubes, out_weight):
    tm_count = lax.axis_size("tm")
    height_count = lax.axis_size("height")
    devices = tm_count * height_count
    width = queries.shape[-1]
    heads = width // HEAD_DIM
    far_count = far_cubes.shape[-1]
    axes = ("tm", "height")
    bf16, f32 = jnp.bfloat16, jnp.float32
    params = pltpu.CompilerParams(vmem_limit_bytes=24 * 2**20)
    alone = pltpu.CompilerParams(vmem_limit_bytes=60 * 2**20)
    anywhere = pl.BlockSpec(memory_space=pltpu.HBM)
    queries_in = queries.reshape(2, 64, width)
    fields_in = keys_values.reshape(2, 2, 64, width)

    first = pl.pallas_call(
        prepare_first,
        in_specs=[anywhere, anywhere, pl.BlockSpec(memory_space=pltpu.VMEM)],
        out_specs=anywhere,
        out_shape=jax.ShapeDtypeStruct((2, 2, height_count, 264, HEAD_DIM), bf16),
        scratch_shapes=[
            pltpu.VMEM((height_count, 2, 64, 3 * HEAD_DIM), bf16),
            pltpu.VMEM((height_count, 2, 2, 64, 3 * HEAD_DIM), bf16),
            pltpu.VMEM((2, 2, height_count, 264, HEAD_DIM), bf16),
            pltpu.SemaphoreType.DMA((3, height_count)),
        ],
        compiler_params=alone,
        name="prepare_first",
    )(queries_in, fields_in, far_cubes.reshape(2, heads, far_count).transpose(0, 2, 1))
    second = pl.pallas_call(
        prepare_second,
        in_specs=[anywhere],
        out_specs=anywhere,
        out_shape=jax.ShapeDtypeStruct((2, 2, height_count, 32, HEAD_DIM), bf16),
        scratch_shapes=[pltpu.SemaphoreType.DMA((2, height_count))],
        compiler_params=alone,
        cost_estimate=pl.CostEstimate(flops=0, bytes_accessed=2**20, transcendentals=0),
        name="prepare_second",
    )(queries_in)

    def exchange(x):
        return lax.all_to_all(x, axes, 0, 0, tiled=True)

    def swap(x, distance):
        return lax.ppermute(x, "tm", [(i, i ^ distance) for i in range(tm_count)])

    def attention(kernel, name, tokens, specs):
        keys = devices * 128
        work = devices * tokens * keys
        return pl.pallas_call(
            functools.partial(kernel, height_count),
            in_specs=specs,
            out_shape=jax.ShapeDtypeStruct((devices, tokens, HEAD_DIM), bf16),
            scratch_shapes=[
                pltpu.VMEM((2, devices, 2, 64, 2 * HEAD_DIM), bf16),
                pltpu.VMEM((devices, tokens, HEAD_DIM), bf16),
                pltpu.VMEM((devices, HEAD_DIM), f32),
                pltpu.SemaphoreType.DMA((5, 4)),
                pltpu.VMEM((ROWS, keys), f32),
                pltpu.VMEM((ROWS, keys), f32),
            ],
            compiler_params=params,
            cost_estimate=pl.CostEstimate(
                flops=8 * work * HEAD_DIM, bytes_accessed=4 * 2**20, transcendentals=work
            ),
            name=name,
        )

    vmem = pl.BlockSpec(memory_space=pltpu.VMEM)
    got_first = exchange(first.reshape(devices, 264, HEAD_DIM))
    got_first, second = lax.optimization_barrier((got_first, second))
    small = got_first[:, 192:256]
    info = got_first[:, 256:264]
    second, small = lax.optimization_barrier((second, small))
    got_second = exchange(second.reshape(devices, 32, HEAD_DIM))
    core_first = swap(got_first, 1)
    chip = swap(small, 2)
    out_large = attention(large_kernel, "attend_large", 64, [anywhere, anywhere, vmem])(
        got_first, core_first, info
    )
    core_chip = swap(chip, 1)

    got_second, out_large = lax.optimization_barrier((got_second, out_large))
    back_large = exchange(out_large)
    out_small = attention(small_kernel, "attend_small", 32, [anywhere] * 5 + [vmem])(
        got_first, got_second, chip, core_first, core_chip, info
    )
    back_large, out_small = lax.optimization_barrier((back_large, out_small))
    back_small = exchange(out_small)
    by_head = out_weight.reshape(height_count, 3, HEAD_DIM, width)
    part = pl.pallas_call(
        project_large,
        in_specs=[vmem, anywhere],
        out_shape=pltpu.VMEM((128, width), f32),
        scratch_shapes=[
            pltpu.VMEM((2, height_count, HEAD_DIM, width), bf16),
            pltpu.SemaphoreType.DMA((2, height_count)),
        ],
        compiler_params=pltpu.CompilerParams(vmem_limit_bytes=50 * 2**20),
        cost_estimate=pl.CostEstimate(
            flops=4 * 128 * width * width // 3, bytes_accessed=14 * 2**20, transcendentals=0
        ),
        name="project_large",
    )(back_large, by_head)
    back_small, part = lax.optimization_barrier((back_small, part))
    output = pl.pallas_call(
        project_small,
        in_specs=[vmem, anywhere, vmem],
        out_shape=jax.ShapeDtypeStruct((128, width), bf16),
        scratch_shapes=[
            pltpu.VMEM((6, height_count, HEAD_DIM, width // 6), bf16),
            pltpu.SemaphoreType.DMA((6, height_count)),
        ],
        compiler_params=pltpu.CompilerParams(vmem_limit_bytes=50 * 2**20),
        cost_estimate=pl.CostEstimate(
            flops=2 * 128 * width * width // 3, bytes_accessed=8 * 2**20, transcendentals=0
        ),
        name="project_small",
    )(back_small, by_head, part)
    return output.reshape(queries.shape)


def solution(mesh):
    in_specs = (
        P("tm", "height", None, None, None),
        P("tm", "height", None, None, None, None),
        P("tm", "height", None, None, None),
        P(),
    )
    out_specs = P("tm", "height", None, None, None)
    fits = mesh.shape["tm"] == 4 and HEADS == 3 * mesh.shape["height"]
    return jax.shard_map(by_heads if fits else body, mesh=mesh, in_specs=in_specs, out_specs=out_specs, check_vma=False)
```

```python
import functools
import math

import jax
import jax.numpy as jnp
import ml_dtypes
import numpy as np
from jax import lax
from jax.experimental import pallas as pl
from jax.experimental.pallas import tpu as pltpu
from jax.sharding import PartitionSpec as P

HEADS = 24
SLOTS = 512
HEAD_DIM = 128
LOG2E = math.log2(math.e)
SCALE = LOG2E / math.sqrt(HEAD_DIM)
TWICE = 1.0 / SCALE
TWICE_HIGH = float(np.asarray(TWICE, ml_dtypes.bfloat16))
TWICE_LOW = TWICE - TWICE_HIGH
ROWS = 512
CHUNK = 512


def padded_2(shard, sides, width):
    for axis, dim in sides:
        peers, length = (lax.axis_size(axis), shard.shape[dim])
        up = [(i, (i + 1) % peers) for i in range(peers - 1)]
        down = [(j, i) for i, j in up]
        last = lax.slice_in_dim(shard, length - width, length, axis=dim)
        leading = lax.slice_in_dim(shard, 0, width, axis=dim)
        before = lax.ppermute(last, axis, up)
        after = lax.ppermute(leading, axis, down)
        shard = jnp.concatenate([before, shard, after], axis=dim)
    return shard


def body(queries, keys_values, far_cubes, out_weight):
    tm_count = lax.axis_size("tm")
    height_count = lax.axis_size("height")
    device_count = tm_count * height_count
    capacity = SLOTS // device_count
    span_time, span_height, span_width, cube, width = queries.shape
    heads = HEADS
    head_size = width // heads
    far_count = far_cubes.shape[-1]
    local_count = span_time * span_height * span_width
    grid_time = span_time * tm_count
    grid_height = span_height * height_count
    far_ids = far_cubes.reshape(local_count, heads, far_count)
    far_time = far_ids // (grid_height * span_width)
    far_height = far_ids // span_width % grid_height
    far_width = far_ids % span_width
    owner_dev = far_time // span_time * height_count + far_height // span_height
    local_cube = (
        far_time % span_time * span_height + far_height % span_height
    ) * span_width + far_width
    tile_code = local_cube * heads + jnp.arange(heads, dtype=jnp.int32)[None, :, None]
    wanted = (
        jnp.zeros((device_count, local_count * heads), jnp.int32).at[owner_dev, tile_code].max(1)
    )
    slot_rank = jnp.cumsum(wanted, axis=1) - 1
    far_slot = owner_dev * capacity + slot_rank[owner_dev, tile_code]
    target = jnp.where(wanted > 0, slot_rank, capacity)
    columns = jnp.broadcast_to(
        jnp.arange(local_count * heads, dtype=jnp.int32)[None, :], wanted.shape
    )
    rows = jnp.broadcast_to(jnp.arange(device_count, dtype=jnp.int32)[:, None], wanted.shape)
    requests = (
        jnp.zeros((device_count, capacity + 1), jnp.int32)
        .at[rows, target]
        .set(columns)[:, :capacity]
    )
    source = keys_values.reshape(local_count, 2, cube, heads, head_size)
    padded = padded_2(keys_values, (("tm", 0), ("height", 1)), 1)
    padded = jnp.pad(padded, ((0, 0), (0, 0), (1, 1), (0, 0), (0, 0), (0, 0)))
    asked = lax.all_to_all(requests, ("tm", "height"), split_axis=0, concat_axis=0, tiled=True)
    tiles = lax.all_to_all(
        source[asked // heads, :, :, asked % heads, :],
        ("tm", "height"),
        split_axis=0,
        concat_axis=0,
        tiled=True,
    )
    received = tiles.reshape(device_count * capacity, 2, cube, head_size)
    first_time = lax.axis_index("tm") * span_time
    first_height = lax.axis_index("height") * span_height
    offsets = jnp.arange(3, dtype=jnp.int32) - 1
    scale = 1.0 / math.sqrt(head_size)
    zero = jnp.zeros((), jnp.int32)
    flat_queries = queries.reshape(local_count, cube, heads, head_size)

    def one_cube(index):
        time_pos = index // (span_height * span_width)
        height_pos = index // span_width % span_height
        width_pos = index % span_width
        window = lax.dynamic_slice(
            padded, (time_pos, height_pos, width_pos, zero, zero, zero), (3, 3, 3, 2, cube, width)
        )
        window = window.reshape(27, 2, cube, heads, head_size)
        global_time = first_time + time_pos + offsets
        global_height = first_height + height_pos + offsets
        global_width = width_pos + offsets
        inside_time = (global_time >= 0) & (global_time < grid_time)
        inside_height = (global_height >= 0) & (global_height < grid_height)
        inside_width = (global_width >= 0) & (global_width < span_width)
        valid = (
            inside_time[:, None, None] & inside_height[None, :, None] & inside_width[None, None, :]
        ).reshape(27)
        keys_window = window[:, 0].reshape(27 * cube, heads, head_size)
        values_window = window[:, 1].reshape(27 * cube, heads, head_size)
        far_tiles = received[far_slot[index]]
        query = flat_queries[index]
        score_window = (
            jnp.einsum("qhd,khd->hqk", query, keys_window, preferred_element_type=jnp.float32)
            * scale
        )
        score_window = jnp.where(jnp.repeat(valid, cube)[None, None, :], score_window, -jnp.inf)
        score_far = (
            jnp.einsum(
                "qhd,hfkd->hqfk", query, far_tiles[:, :, 0], preferred_element_type=jnp.float32
            )
            * scale
        )
        scores = jnp.concatenate(
            [score_window, score_far.reshape(heads, cube, far_count * cube)], axis=-1
        )
        largest = jnp.max(scores, axis=-1, keepdims=True)
        lifted = jnp.exp(scores - largest)
        weights = (lifted / jnp.sum(lifted, axis=-1, keepdims=True)).astype(jnp.bfloat16)
        attended = jnp.einsum(
            "hqk,khd->qhd",
            weights[:, :, : 27 * cube],
            values_window,
            preferred_element_type=jnp.float32,
        )
        far_weights = weights[:, :, 27 * cube :].reshape(heads, cube, far_count, cube)
        attended = attended + jnp.einsum(
            "hqfk,hfkd->qhd", far_weights, far_tiles[:, :, 1], preferred_element_type=jnp.float32
        )
        return attended.reshape(cube, width).astype(jnp.bfloat16)

    attended = lax.map(one_cube, jnp.arange(local_count, dtype=jnp.int32))
    output = jnp.dot(
        attended.reshape(local_count * cube, width), out_weight, preferred_element_type=jnp.float32
    )
    return output.astype(jnp.bfloat16).reshape(queries.shape)


def head_lanes(head):
    return slice(head * HEAD_DIM, (head + 1) * HEAD_DIM)


def list_counts(far_ref, w, head):
    cubes = lax.broadcasted_iota(jnp.int32, (far_ref.shape[1], HEAD_DIM), 1) % 64
    listed = (far_ref[w, :, head : head + 1] == cubes).astype(jnp.float32)
    return jnp.sum(listed, axis=0, keepdims=True).astype(jnp.bfloat16)


def prepare_first(q_ref, kv_ref, far_ref, out_ref, q_in, kv_in, far_in, staged, sems, far_sem):
    groups = out_ref.shape[2]
    span = 3 * HEAD_DIM

    def copies_in(g):
        lanes = pl.ds(g * span, span)
        return (
            pltpu.make_async_copy(q_ref.at[:, :, lanes], q_in.at[g], sems.at[0, g]),
            pltpu.make_async_copy(kv_ref.at[:, :, :, lanes], kv_in.at[g], sems.at[1, g]),
        )

    def copy_out(g):
        return pltpu.make_async_copy(staged.at[:, :, g], out_ref.at[:, :, g], sems.at[2, g])

    far_copy = pltpu.make_async_copy(far_ref, far_in, far_sem)
    far_copy.start()
    for g in range(groups):
        for copy in copies_in(g):
            copy.start()
    far_copy.wait()
    for g in range(groups):
        for core in range(2):
            for chip in range(2):
                counts = list_counts(far_in, core, 3 * g + 2 * chip)
                staged[chip, core, g, 256:264, :] = jnp.broadcast_to(counts, (8, HEAD_DIM))
    for g in range(groups):
        for copy in copies_in(g):
            copy.wait()
        for core in range(2):
            for chip in range(2):
                lanes = head_lanes(2 * chip)
                staged[chip, core, g, 0:64, :] = q_in[g, core, :, lanes]
                staged[chip, core, g, 64:128, :] = kv_in[g, core, 0, :, lanes]
                staged[chip, core, g, 128:192, :] = kv_in[g, core, 1, :, lanes]
                staged[chip, core, g, 192:256, :] = kv_in[g, core, chip, :, head_lanes(1)]
        copy_out(g).start()
    for g in range(groups):
        copy_out(g).wait()


def prepare_second(q_ref, far_ref, out_ref, q_in, staged, sems, out_sem):
    groups = out_ref.shape[0]
    copies = [
        pltpu.make_async_copy(
            q_ref.at[:, :, pl.ds((3 * g + 1) * HEAD_DIM, HEAD_DIM)], q_in.at[g], sems.at[g]
        )
        for g in range(groups)
    ]
    for copy in copies:
        copy.start()
    top_row = lax.broadcasted_iota(jnp.int32, (8, HEAD_DIM), 0) == 0
    for g in range(groups):
        counts = [list_counts(far_ref, w, 3 * g + 1).astype(jnp.float32) for w in range(2)]
        staged[g, 128:136, :] = jnp.where(top_row, *counts).astype(jnp.bfloat16)
        copies[g].wait()
        staged[g, 0:64, :] = q_in[g, 0]
        staged[g, 64:128, :] = q_in[g, 1]
    copy = pltpu.make_async_copy(staged, out_ref, out_sem)
    copy.start()
    copy.wait()


def set_constants(listed, time, height, bias_ref, height_count):
    lane = lax.broadcasted_iota(jnp.int32, listed.shape, 1)
    place = lane % 64 // 2
    near = (jnp.abs(time - place // height_count) <= 1) & (
        jnp.abs(height - place % height_count) <= 1
    )
    counts = listed + jnp.where(near, 1.0, 0.0)
    high = lane < 64
    bias_ref[...] = jnp.where(
        counts < 0.5,
        jnp.where(high, -1e30, 0.0),
        jnp.where(counts > 1.5, jnp.where(high, TWICE_HIGH, TWICE_LOW), 0.0),
    )


def set_margins(kv_ref):
    shape = (2, 64, HEAD_DIM)
    width = lax.broadcasted_iota(jnp.int32, shape, 0)
    lane = lax.broadcasted_iota(jnp.int32, shape, 2) % 64
    for s in range(kv_ref.shape[1]):
        kv_ref[0, s, :, :, HEAD_DIM:] = (lane == 2 * s + width).astype(jnp.bfloat16)
        kv_ref[1, s, :, :, HEAD_DIM:] = jnp.ones(shape, jnp.bfloat16)


def attend(q_at, wait_values, kv_ref, bias_ref, out_ref, out_in, out_sems, scores):
    sources, tokens = bias_ref.shape[0], 64
    step = ROWS // tokens
    chunk = CHUNK // 128
    chunks = range(0, kv_ref.shape[1], chunk)
    fold = out_ref.shape[1] // tokens

    def copy_out(first):
        at = pl.ds(first // fold, step // fold)
        return pltpu.make_async_copy(out_in.at[at], out_ref.at[at], out_sems.at[first // step])

    def score(first, s_ref):
        bias = [
            jnp.broadcast_to(bias_ref[pl.ds(first + i, 1), :], (tokens, HEAD_DIM))
            for i in range(step)
        ]
        bias = jnp.concatenate(bias, axis=0).astype(jnp.bfloat16)
        query = jnp.concatenate([q_at(first, step), bias], axis=1)
        top = None
        for s in chunks:
            part = lax.dot_general(
                query,
                kv_ref[0, s : s + chunk].reshape(CHUNK, 2 * HEAD_DIM),
                (((1,), (1,)), ((), ())),
                preferred_element_type=jnp.float32,
            )
            s_ref[:, s * 128 : s * 128 + CHUNK] = part
            for lane in range(0, CHUNK, HEAD_DIM):
                piece = part[:, lane : lane + HEAD_DIM]
                top = piece if top is None else jnp.maximum(top, piece)
        return jnp.max(top, axis=1, keepdims=True)

    def mix(first, s_ref, largest):
        mixed = jnp.zeros((ROWS, 2 * HEAD_DIM), jnp.float32)
        for s in chunks:
            lifted = jnp.exp2((s_ref[:, s * 128 : s * 128 + CHUNK] - largest) * SCALE)
            mixed += jnp.dot(
                lifted.astype(jnp.bfloat16),
                kv_ref[1, s : s + chunk].reshape(CHUNK, 2 * HEAD_DIM),
                preferred_element_type=jnp.float32,
            )
        result = (mixed[:, :HEAD_DIM] / mixed[:, HEAD_DIM:]).astype(out_ref.dtype)
        at = pl.ds(first // fold, step // fold)
        out_in[at] = result.reshape(step // fold, fold * tokens, HEAD_DIM)
        copy_out(first).start()

    def two_blocks(index, largest):
        first = index * 2 * step
        later = score(first + step, scores[1])
        mix(first, scores[0], largest)
        largest = score(first + 2 * step, scores[0])
        mix(first + step, scores[1], later)
        return largest

    largest = score(0, scores[0])
    wait_values()
    largest = lax.fori_loop(0, sources // step // 2 - 1, two_blocks, largest)
    last = sources - step
    later = score(last, scores[1])
    mix(last - step, scores[0], largest)
    mix(last, scores[1], later)
    for first in range(0, sources, step):
        copy_out(first).wait()


def pieces(count, source, target, sems, row):
    part = count // 2
    return [
        pltpu.make_async_copy(
            source(pl.ds(i * part, part)), target(pl.ds(i * part, part)), sems.at[row, i]
        )
        for i in range(2)
    ]


def large_kernel(
    height_count, mine_ref, core_ref, info_ref, out_ref, kv_ref, q_in, info_in, out_in, bias_ref,
    sems, out_sems, info_sem, *scores
):
    core = lax.axis_index("tm") % 2
    count = mine_ref.shape[0]
    own = [
        pieces(
            count,
            lambda at, k=k: mine_ref.at[at, 64 + 64 * k : 128 + 64 * k, :],
            lambda at, k=k: kv_ref.at[k, at, core, :, 0:HEAD_DIM],
            sems,
            k,
        )
        for k in range(2)
    ]
    other = [
        pieces(
            count,
            lambda at, k=k: core_ref.at[at, 64 + 64 * k : 128 + 64 * k, :],
            lambda at, k=k: kv_ref.at[k, at, 1 - core, :, 0:HEAD_DIM],
            sems,
            2 + k,
        )
        for k in range(2)
    ]
    query = pieces(count, lambda at: mine_ref.at[at, 0:64, :], lambda at: q_in.at[at], sems, 4)
    for copy in own[0] + other[0] + query + own[1] + other[1]:
        copy.start()
    info_copy = pltpu.make_async_copy(info_ref, info_in, info_sem)
    info_copy.start()
    set_margins(kv_ref)
    info_copy.wait()
    listed = info_in[:, 0, :].astype(jnp.float32)
    source = lax.broadcasted_iota(jnp.int32, listed.shape, 0)
    set_constants(listed, source // height_count, source % height_count, bias_ref, height_count)
    for copy in own[0] + other[0] + query:
        copy.wait()

    def wait_values():
        for copy in own[1] + other[1]:
            copy.wait()

    def q_at(first, count):
        return q_in[pl.ds(first, count)].reshape(count * 64, HEAD_DIM)

    attend(q_at, wait_values, kv_ref, bias_ref, out_ref, out_in, out_sems, scores)


def small_kernel(
    height_count, first_ref, second_ref, chip_ref, core_first_ref, core_chip_ref, info_ref, out_ref,
    kv_ref, q_in, info_in, out_in, bias_ref, sems, out_sems, info_sem, *scores
):
    core = lax.axis_index("tm") % 2
    chip = lax.axis_index("tm") // 2
    count = first_ref.shape[0]

    def kept(source, kind, width, row):
        return pieces(
            count, source, lambda at: kv_ref.at[kind, at, width, :, 0:HEAD_DIM], sems, row
        )

    copies = pieces(
        height_count, lambda at: second_ref.at[at, 0:128, :], lambda at: q_in.at[at], sems, 4
    )
    copies += kept(lambda at: first_ref.at[at, 192:256, :], chip, core, 0)
    copies += kept(lambda at: chip_ref.at[at], 1 - chip, core, 1)
    copies += kept(lambda at: core_first_ref.at[at, 192:256, :], chip, 1 - core, 2)
    copies += kept(lambda at: core_chip_ref.at[at], 1 - chip, 1 - core, 3)
    for copy in copies:
        copy.start()
    info_copy = pltpu.make_async_copy(info_ref, info_in, info_sem)
    info_copy.start()
    set_margins(kv_ref)
    info_copy.wait()
    listed = info_in[:, 0:2, :].astype(jnp.float32).reshape(2 * height_count, HEAD_DIM)
    source = lax.broadcasted_iota(jnp.int32, listed.shape, 0)
    set_constants(listed, lax.axis_index("tm"), source // 2, bias_ref, height_count)
    for copy in copies:
        copy.wait()

    def q_at(first, count):
        return q_in[pl.ds(first // 2, count // 2)].reshape(count * 64, HEAD_DIM)

    attend(q_at, lambda: None, kv_ref, bias_ref, out_ref, out_in, out_sems, scores)


def side_by_side(refs, rows):
    return jnp.concatenate([jnp.concatenate([refs[i] for i in row], axis=1) for row in rows], axis=0)


def project_large(back_ref, weight_ref, part_ref, weights, sems):
    groups = back_ref.shape[0] // 4

    def copies(g):
        return [
            pltpu.make_async_copy(weight_ref.at[g, 2 * chip], weights.at[chip, g], sems.at[chip, g])
            for chip in range(2)
        ]

    for g in range(groups):
        for copy in copies(g):
            copy.start()
    total = None
    for g in range(0, groups, 2):
        for copy in copies(g) + copies(g + 1):
            copy.wait()
        for chip in range(2):
            first = chip * 2 * groups + g
            rows = [[first + core * groups + i for i in range(2)] for core in range(2)]
            part = jnp.dot(
                side_by_side(back_ref, rows),
                weights[chip, g : g + 2].reshape(2 * HEAD_DIM, weights.shape[-1]),
                preferred_element_type=jnp.float32,
            )
            total = part if total is None else total + part
    part_ref[...] = total


def project_small(
    back_ref, weight_ref, part_ref, out_ref, weights, back_in, out_in, sems, out_sems, back_sem
):
    groups = back_ref.shape[0]
    tiles = sems.shape[0]
    tile = weights.shape[-1]

    def copy_in(n):
        lanes = slice(n * tile, (n + 1) * tile)
        return pltpu.make_async_copy(weight_ref.at[:, 1, :, lanes], weights.at[n], sems.at[n])

    back_copy = pltpu.make_async_copy(back_ref, back_in, back_sem)
    back_copy.start()
    for n in range(tiles):
        copy_in(n).start()
    back_copy.wait()
    attended = side_by_side(back_in, [range(groups)])
    copies_out = []
    for n in range(tiles):
        copy_in(n).wait()
        lanes = slice(n * tile, (n + 1) * tile)
        total = part_ref[:, lanes] + jnp.dot(
            attended,
            weights[n].reshape(groups * HEAD_DIM, tile),
            preferred_element_type=jnp.float32,
        )
        out_in[:, lanes] = total.astype(out_ref.dtype)
        copy = pltpu.make_async_copy(out_in.at[:, lanes], out_ref.at[:, lanes], out_sems.at[n])
        copy.start()
        copies_out.append(copy)
    for copy in copies_out:
        copy.wait()


def by_heads(queries, keys_values, far_cubes, out_weight):
    tm_count = lax.axis_size("tm")
    height_count = lax.axis_size("height")
    devices = tm_count * height_count
    width = queries.shape[-1]
    heads = width // HEAD_DIM
    far_count = far_cubes.shape[-1]
    axes = ("tm", "height")
    bf16, f32 = jnp.bfloat16, jnp.float32
    params = pltpu.CompilerParams(vmem_limit_bytes=36 * 2**20)
    alone = pltpu.CompilerParams(vmem_limit_bytes=60 * 2**20)
    anywhere = pl.BlockSpec(memory_space=pltpu.HBM)
    queries_in = queries.reshape(2, 64, width)
    fields_in = keys_values.reshape(2, 2, 64, width)

    far_lists = far_cubes.reshape(2, heads, far_count).transpose(0, 2, 1)

    first = pl.pallas_call(
        prepare_first,
        in_specs=[anywhere, anywhere, anywhere],
        out_specs=anywhere,
        out_shape=jax.ShapeDtypeStruct((2, 2, height_count, 264, HEAD_DIM), bf16),
        scratch_shapes=[
            pltpu.VMEM((height_count, 2, 64, 3 * HEAD_DIM), bf16),
            pltpu.VMEM((height_count, 2, 2, 64, 3 * HEAD_DIM), bf16),
            pltpu.VMEM((2, far_count, heads), jnp.int32),
            pltpu.VMEM((2, 2, height_count, 264, HEAD_DIM), bf16),
            pltpu.SemaphoreType.DMA((3, height_count)),
            pltpu.SemaphoreType.DMA,
        ],
        compiler_params=alone,
        name="prepare_first",
    )(queries_in, fields_in, far_lists)
    second = pl.pallas_call(
        prepare_second,
        in_specs=[anywhere, pl.BlockSpec(memory_space=pltpu.VMEM)],
        out_specs=anywhere,
        out_shape=jax.ShapeDtypeStruct((height_count, 136, HEAD_DIM), bf16),
        scratch_shapes=[
            pltpu.VMEM((height_count, 2, 64, HEAD_DIM), bf16),
            pltpu.VMEM((height_count, 136, HEAD_DIM), bf16),
            pltpu.SemaphoreType.DMA((height_count,)),
            pltpu.SemaphoreType.DMA,
        ],
        compiler_params=alone,
        cost_estimate=pl.CostEstimate(flops=0, bytes_accessed=2**21, transcendentals=0),
        name="prepare_second",
    )(queries_in, far_lists)

    def exchange(x, over=axes):
        return lax.all_to_all(x, over, 0, 0, tiled=True)

    def swap(x, distance):
        return lax.ppermute(x, "tm", [(i, i ^ distance) for i in range(tm_count)])

    def attention(kernel, name, cubes, shape, operands):
        keys = devices * 128
        work = cubes * 64 * keys
        return pl.pallas_call(
            functools.partial(kernel, height_count),
            in_specs=[anywhere] * operands,
            out_specs=anywhere,
            out_shape=jax.ShapeDtypeStruct(shape, bf16),
            scratch_shapes=[
                pltpu.VMEM((2, devices, 2, 64, 2 * HEAD_DIM), bf16),
                pltpu.VMEM(shape, bf16),
                pltpu.VMEM((shape[0], 8, HEAD_DIM), bf16),
                pltpu.VMEM(shape, bf16),
                pltpu.VMEM((cubes, HEAD_DIM), f32),
                pltpu.SemaphoreType.DMA((5, 4)),
                pltpu.SemaphoreType.DMA((cubes * 64 // ROWS,)),
                pltpu.SemaphoreType.DMA,
                pltpu.VMEM((ROWS, keys), f32),
                pltpu.VMEM((ROWS, keys), f32),
            ],
            compiler_params=params,
            cost_estimate=pl.CostEstimate(
                flops=8 * work * HEAD_DIM, bytes_accessed=4 * 2**20, transcendentals=work
            ),
            name=name,
        )

    vmem = pl.BlockSpec(memory_space=pltpu.VMEM)
    got_first = exchange(first.reshape(devices, 264, HEAD_DIM))
    got_first, second = lax.optimization_barrier((got_first, second))
    small = got_first[:, 192:256]
    info = got_first[:, 256:264]
    second, small = lax.optimization_barrier((second, small))
    got_second = exchange(second, "height")
    core_first = swap(got_first, 1)
    chip = swap(small, 2)
    out_large = attention(large_kernel, "attend_large", devices, (devices, 64, HEAD_DIM), 3)(
        got_first, core_first, info
    )
    core_chip = swap(chip, 1)

    got_second, out_large = lax.optimization_barrier((got_second, out_large))
    back_large = exchange(out_large)
    out_small = attention(small_kernel, "attend_small", 2 * height_count, (height_count, 128, HEAD_DIM), 6)(
        got_first, got_second, chip, core_first, core_chip, got_second[:, 128:136]
    )
    back_large, out_small = lax.optimization_barrier((back_large, out_small))
    back_small = exchange(out_small, "height")
    by_head = out_weight.reshape(height_count, 3, HEAD_DIM, width)
    part = pl.pallas_call(
        project_large,
        in_specs=[vmem, anywhere],
        out_shape=pltpu.VMEM((128, width), f32),
        scratch_shapes=[
            pltpu.VMEM((2, height_count, HEAD_DIM, width), bf16),
            pltpu.SemaphoreType.DMA((2, height_count)),
        ],
        compiler_params=pltpu.CompilerParams(vmem_limit_bytes=50 * 2**20),
        cost_estimate=pl.CostEstimate(
            flops=4 * 128 * width * width // 3, bytes_accessed=14 * 2**20, transcendentals=0
        ),
        name="project_large",
    )(back_large, by_head)
    back_small, part = lax.optimization_barrier((back_small, part))
    output = pl.pallas_call(
        project_small,
        in_specs=[anywhere, anywhere, vmem],
        out_specs=anywhere,
        out_shape=jax.ShapeDtypeStruct((128, width), bf16),
        scratch_shapes=[
            pltpu.VMEM((6, height_count, HEAD_DIM, width // 6), bf16),
            pltpu.VMEM(back_small.shape, bf16),
            pltpu.VMEM((128, width), bf16),
            pltpu.SemaphoreType.DMA((6,)),
            pltpu.SemaphoreType.DMA((6,)),
            pltpu.SemaphoreType.DMA,
        ],
        compiler_params=pltpu.CompilerParams(vmem_limit_bytes=50 * 2**20),
        cost_estimate=pl.CostEstimate(
            flops=2 * 128 * width * width // 3, bytes_accessed=8 * 2**20, transcendentals=0
        ),
        name="project_small",
    )(back_small, by_head, part)
    return output.reshape(queries.shape)


def solution(mesh):
    in_specs = (
        P("tm", "height", None, None, None),
        P("tm", "height", None, None, None, None),
        P("tm", "height", None, None, None),
        P(),
    )
    out_specs = P("tm", "height", None, None, None)
    fits = mesh.shape["tm"] == 4 and HEADS == 3 * mesh.shape["height"]
    return jax.shard_map(by_heads if fits else body, mesh=mesh, in_specs=in_specs, out_specs=out_specs, check_vma=False)
```

```python
import functools
import math

import jax
import jax.numpy as jnp
import ml_dtypes
import numpy as np
from jax import lax
from jax.experimental import pallas as pl
from jax.experimental.pallas import tpu as pltpu
from jax.sharding import PartitionSpec as P

HEADS = 24
SLOTS = 512
HEAD_DIM = 128
LOG2E = math.log2(math.e)
SCALE = LOG2E / math.sqrt(HEAD_DIM)
TWICE = 1.0 / SCALE
TWICE_HIGH = float(np.asarray(TWICE, ml_dtypes.bfloat16))
TWICE_LOW = TWICE - TWICE_HIGH
ROWS = 512
CHUNK = 512


def padded_2(shard, sides, width):
    for axis, dim in sides:
        peers, length = (lax.axis_size(axis), shard.shape[dim])
        up = [(i, (i + 1) % peers) for i in range(peers - 1)]
        down = [(j, i) for i, j in up]
        last = lax.slice_in_dim(shard, length - width, length, axis=dim)
        leading = lax.slice_in_dim(shard, 0, width, axis=dim)
        before = lax.ppermute(last, axis, up)
        after = lax.ppermute(leading, axis, down)
        shard = jnp.concatenate([before, shard, after], axis=dim)
    return shard


def body(queries, keys_values, far_cubes, out_weight):
    tm_count = lax.axis_size("tm")
    height_count = lax.axis_size("height")
    device_count = tm_count * height_count
    capacity = SLOTS // device_count
    span_time, span_height, span_width, cube, width = queries.shape
    heads = HEADS
    head_size = width // heads
    far_count = far_cubes.shape[-1]
    local_count = span_time * span_height * span_width
    grid_time = span_time * tm_count
    grid_height = span_height * height_count
    far_ids = far_cubes.reshape(local_count, heads, far_count)
    far_time = far_ids // (grid_height * span_width)
    far_height = far_ids // span_width % grid_height
    far_width = far_ids % span_width
    owner_dev = far_time // span_time * height_count + far_height // span_height
    local_cube = (
        far_time % span_time * span_height + far_height % span_height
    ) * span_width + far_width
    tile_code = local_cube * heads + jnp.arange(heads, dtype=jnp.int32)[None, :, None]
    wanted = (
        jnp.zeros((device_count, local_count * heads), jnp.int32).at[owner_dev, tile_code].max(1)
    )
    slot_rank = jnp.cumsum(wanted, axis=1) - 1
    far_slot = owner_dev * capacity + slot_rank[owner_dev, tile_code]
    target = jnp.where(wanted > 0, slot_rank, capacity)
    columns = jnp.broadcast_to(
        jnp.arange(local_count * heads, dtype=jnp.int32)[None, :], wanted.shape
    )
    rows = jnp.broadcast_to(jnp.arange(device_count, dtype=jnp.int32)[:, None], wanted.shape)
    requests = (
        jnp.zeros((device_count, capacity + 1), jnp.int32)
        .at[rows, target]
        .set(columns)[:, :capacity]
    )
    source = keys_values.reshape(local_count, 2, cube, heads, head_size)
    padded = padded_2(keys_values, (("tm", 0), ("height", 1)), 1)
    padded = jnp.pad(padded, ((0, 0), (0, 0), (1, 1), (0, 0), (0, 0), (0, 0)))
    asked = lax.all_to_all(requests, ("tm", "height"), split_axis=0, concat_axis=0, tiled=True)
    tiles = lax.all_to_all(
        source[asked // heads, :, :, asked % heads, :],
        ("tm", "height"),
        split_axis=0,
        concat_axis=0,
        tiled=True,
    )
    received = tiles.reshape(device_count * capacity, 2, cube, head_size)
    first_time = lax.axis_index("tm") * span_time
    first_height = lax.axis_index("height") * span_height
    offsets = jnp.arange(3, dtype=jnp.int32) - 1
    scale = 1.0 / math.sqrt(head_size)
    zero = jnp.zeros((), jnp.int32)
    flat_queries = queries.reshape(local_count, cube, heads, head_size)

    def one_cube(index):
        time_pos = index // (span_height * span_width)
        height_pos = index // span_width % span_height
        width_pos = index % span_width
        window = lax.dynamic_slice(
            padded, (time_pos, height_pos, width_pos, zero, zero, zero), (3, 3, 3, 2, cube, width)
        )
        window = window.reshape(27, 2, cube, heads, head_size)
        global_time = first_time + time_pos + offsets
        global_height = first_height + height_pos + offsets
        global_width = width_pos + offsets
        inside_time = (global_time >= 0) & (global_time < grid_time)
        inside_height = (global_height >= 0) & (global_height < grid_height)
        inside_width = (global_width >= 0) & (global_width < span_width)
        valid = (
            inside_time[:, None, None] & inside_height[None, :, None] & inside_width[None, None, :]
        ).reshape(27)
        keys_window = window[:, 0].reshape(27 * cube, heads, head_size)
        values_window = window[:, 1].reshape(27 * cube, heads, head_size)
        far_tiles = received[far_slot[index]]
        query = flat_queries[index]
        score_window = (
            jnp.einsum("qhd,khd->hqk", query, keys_window, preferred_element_type=jnp.float32)
            * scale
        )
        score_window = jnp.where(jnp.repeat(valid, cube)[None, None, :], score_window, -jnp.inf)
        score_far = (
            jnp.einsum(
                "qhd,hfkd->hqfk", query, far_tiles[:, :, 0], preferred_element_type=jnp.float32
            )
            * scale
        )
        scores = jnp.concatenate(
            [score_window, score_far.reshape(heads, cube, far_count * cube)], axis=-1
        )
        largest = jnp.max(scores, axis=-1, keepdims=True)
        lifted = jnp.exp(scores - largest)
        weights = (lifted / jnp.sum(lifted, axis=-1, keepdims=True)).astype(jnp.bfloat16)
        attended = jnp.einsum(
            "hqk,khd->qhd",
            weights[:, :, : 27 * cube],
            values_window,
            preferred_element_type=jnp.float32,
        )
        far_weights = weights[:, :, 27 * cube :].reshape(heads, cube, far_count, cube)
        attended = attended + jnp.einsum(
            "hqfk,hfkd->qhd", far_weights, far_tiles[:, :, 1], preferred_element_type=jnp.float32
        )
        return attended.reshape(cube, width).astype(jnp.bfloat16)

    attended = lax.map(one_cube, jnp.arange(local_count, dtype=jnp.int32))
    output = jnp.dot(
        attended.reshape(local_count * cube, width), out_weight, preferred_element_type=jnp.float32
    )
    return output.astype(jnp.bfloat16).reshape(queries.shape)


def head_lanes(head):
    return slice(head * HEAD_DIM, (head + 1) * HEAD_DIM)


def list_counts(far_ref, w, head):
    cubes = lax.broadcasted_iota(jnp.int32, (far_ref.shape[1], HEAD_DIM), 1) % 64
    listed = (far_ref[w, :, head : head + 1] == cubes).astype(jnp.float32)
    return jnp.sum(listed, axis=0, keepdims=True).astype(jnp.bfloat16)


def prepare_first(q_ref, kv_ref, far_ref, out_ref, q_in, kv_in, far_in, staged, sems, far_sem):
    groups = out_ref.shape[2]

    def copies_in(core):
        return [
            pltpu.make_async_copy(q_ref.at[core], q_in.at[core], sems.at[core, 0]),
            pltpu.make_async_copy(kv_ref.at[core, 0], kv_in.at[core, 0], sems.at[core, 1]),
            pltpu.make_async_copy(kv_ref.at[core, 1], kv_in.at[core, 1], sems.at[core, 2]),
        ]

    def copy_out(chip, core):
        return pltpu.make_async_copy(
            staged.at[chip, core], out_ref.at[chip, core], sems.at[core, 3 + chip]
        )

    far_copy = pltpu.make_async_copy(far_ref, far_in, far_sem)
    far_copy.start()
    for core in range(2):
        for copy in copies_in(core):
            copy.start()
    far_copy.wait()
    for core in range(2):
        for chip in range(2):
            for g in range(groups):
                counts = list_counts(far_in, core, 3 * g + 2 * chip)
                staged[chip, core, g, 256:264, :] = jnp.broadcast_to(counts, (8, HEAD_DIM))
    for core in range(2):
        for copy in copies_in(core):
            copy.wait()
        for chip in range(2):
            for g in range(groups):
                lanes = head_lanes(3 * g + 2 * chip)
                staged[chip, core, g, 0:64, :] = q_in[core, :, lanes]
                staged[chip, core, g, 64:128, :] = kv_in[core, 0, :, lanes]
                staged[chip, core, g, 128:192, :] = kv_in[core, 1, :, lanes]
                staged[chip, core, g, 192:256, :] = kv_in[core, chip, :, head_lanes(3 * g + 1)]
            copy_out(chip, core).start()
    for core in range(2):
        for chip in range(2):
            copy_out(chip, core).wait()


def prepare_second(q_ref, far_ref, out_ref, q_in, staged, sems, out_sem):
    groups = out_ref.shape[0]
    copies = [
        pltpu.make_async_copy(
            q_ref.at[:, :, pl.ds((3 * g + 1) * HEAD_DIM, HEAD_DIM)], q_in.at[g], sems.at[g]
        )
        for g in range(groups)
    ]
    for copy in copies:
        copy.start()
    top_row = lax.broadcasted_iota(jnp.int32, (8, HEAD_DIM), 0) == 0
    for g in range(groups):
        counts = [list_counts(far_ref, w, 3 * g + 1).astype(jnp.float32) for w in range(2)]
        staged[g, 128:136, :] = jnp.where(top_row, *counts).astype(jnp.bfloat16)
        copies[g].wait()
        staged[g, 0:64, :] = q_in[g, 0]
        staged[g, 64:128, :] = q_in[g, 1]
    copy = pltpu.make_async_copy(staged, out_ref, out_sem)
    copy.start()
    copy.wait()


def set_constants(listed, time, height, bias_ref, height_count):
    lane = lax.broadcasted_iota(jnp.int32, listed.shape, 1)
    place = lane % 64 // 2
    near = (jnp.abs(time - place // height_count) <= 1) & (
        jnp.abs(height - place % height_count) <= 1
    )
    counts = listed + jnp.where(near, 1.0, 0.0)
    high = lane < 64
    bias_ref[...] = jnp.where(
        counts < 0.5,
        jnp.where(high, -1e30, 0.0),
        jnp.where(counts > 1.5, jnp.where(high, TWICE_HIGH, TWICE_LOW), 0.0),
    )


def set_margins(kv_ref):
    shape = (2, 64, HEAD_DIM)
    width = lax.broadcasted_iota(jnp.int32, shape, 0)
    lane = lax.broadcasted_iota(jnp.int32, shape, 2) % 64
    for s in range(kv_ref.shape[1]):
        kv_ref[0, s, :, :, HEAD_DIM:] = (lane == 2 * s + width).astype(jnp.bfloat16)
        kv_ref[1, s, :, :, HEAD_DIM:] = jnp.ones(shape, jnp.bfloat16)


def attend(q_at, wait_values, kv_ref, bias_ref, out_ref, out_in, out_sems, scores):
    sources, tokens = bias_ref.shape[0], 64
    step = ROWS // tokens
    chunk = CHUNK // 128
    chunks = range(0, kv_ref.shape[1], chunk)
    fold = out_ref.shape[1] // tokens

    def copy_out(first):
        at = pl.ds(first // fold, step // fold)
        return pltpu.make_async_copy(out_in.at[at], out_ref.at[at], out_sems.at[first // step])

    def score(first, s_ref):
        bias = [
            jnp.broadcast_to(bias_ref[pl.ds(first + i, 1), :], (tokens, HEAD_DIM))
            for i in range(step)
        ]
        bias = jnp.concatenate(bias, axis=0).astype(jnp.bfloat16)
        query = jnp.concatenate([q_at(first, step), bias], axis=1)
        top = None
        for s in chunks:
            part = lax.dot_general(
                query,
                kv_ref[0, s : s + chunk].reshape(CHUNK, 2 * HEAD_DIM),
                (((1,), (1,)), ((), ())),
                preferred_element_type=jnp.float32,
            )
            s_ref[:, s * 128 : s * 128 + CHUNK] = part
            for lane in range(0, CHUNK, HEAD_DIM):
                piece = part[:, lane : lane + HEAD_DIM]
                top = piece if top is None else jnp.maximum(top, piece)
        return jnp.max(top, axis=1, keepdims=True)

    def mix(first, s_ref, largest):
        mixed = jnp.zeros((ROWS, 2 * HEAD_DIM), jnp.float32)
        for s in chunks:
            lifted = jnp.exp2((s_ref[:, s * 128 : s * 128 + CHUNK] - largest) * SCALE)
            mixed += jnp.dot(
                lifted.astype(jnp.bfloat16),
                kv_ref[1, s : s + chunk].reshape(CHUNK, 2 * HEAD_DIM),
                preferred_element_type=jnp.float32,
            )
        result = (mixed[:, :HEAD_DIM] / mixed[:, HEAD_DIM:]).astype(out_ref.dtype)
        at = pl.ds(first // fold, step // fold)
        out_in[at] = result.reshape(step // fold, fold * tokens, HEAD_DIM)
        copy_out(first).start()

    def two_blocks(index, largest):
        first = index * 2 * step
        later = score(first + step, scores[1])
        mix(first, scores[0], largest)
        largest = score(first + 2 * step, scores[0])
        mix(first + step, scores[1], later)
        return largest

    largest = score(0, scores[0])
    wait_values()
    largest = lax.fori_loop(0, sources // step // 2 - 1, two_blocks, largest)
    last = sources - step
    later = score(last, scores[1])
    mix(last - step, scores[0], largest)
    mix(last, scores[1], later)
    for first in range(0, sources, step):
        copy_out(first).wait()


def pieces(count, source, target, sems, row):
    part = count // 2
    return [
        pltpu.make_async_copy(
            source(pl.ds(i * part, part)), target(pl.ds(i * part, part)), sems.at[row, i]
        )
        for i in range(2)
    ]


def large_kernel(
    height_count, mine_ref, core_ref, info_ref, out_ref, kv_ref, q_in, info_in, out_in, bias_ref,
    sems, out_sems, info_sem, *scores
):
    core = lax.axis_index("tm") % 2
    count = mine_ref.shape[0]
    own = [
        pieces(
            count,
            lambda at, k=k: mine_ref.at[at, 64 + 64 * k : 128 + 64 * k, :],
            lambda at, k=k: kv_ref.at[k, at, core, :, 0:HEAD_DIM],
            sems,
            k,
        )
        for k in range(2)
    ]
    other = [
        pieces(
            count,
            lambda at, k=k: core_ref.at[at, 64 + 64 * k : 128 + 64 * k, :],
            lambda at, k=k: kv_ref.at[k, at, 1 - core, :, 0:HEAD_DIM],
            sems,
            2 + k,
        )
        for k in range(2)
    ]
    query = pieces(count, lambda at: mine_ref.at[at, 0:64, :], lambda at: q_in.at[at], sems, 4)
    for copy in own[0] + other[0] + query + own[1] + other[1]:
        copy.start()
    info_copy = pltpu.make_async_copy(info_ref, info_in, info_sem)
    info_copy.start()
    set_margins(kv_ref)
    info_copy.wait()
    listed = info_in[:, 0, :].astype(jnp.float32)
    source = lax.broadcasted_iota(jnp.int32, listed.shape, 0)
    set_constants(listed, source // height_count, source % height_count, bias_ref, height_count)
    for copy in own[0] + other[0] + query:
        copy.wait()

    def wait_values():
        for copy in own[1] + other[1]:
            copy.wait()

    def q_at(first, count):
        return q_in[pl.ds(first, count)].reshape(count * 64, HEAD_DIM)

    attend(q_at, wait_values, kv_ref, bias_ref, out_ref, out_in, out_sems, scores)


def small_kernel(
    height_count, first_ref, second_ref, chip_ref, core_first_ref, core_chip_ref, info_ref, out_ref,
    kv_ref, q_in, info_in, out_in, bias_ref, sems, out_sems, info_sem, *scores
):
    core = lax.axis_index("tm") % 2
    chip = lax.axis_index("tm") // 2
    count = first_ref.shape[0]

    def kept(source, kind, width, row):
        return pieces(
            count, source, lambda at: kv_ref.at[kind, at, width, :, 0:HEAD_DIM], sems, row
        )

    copies = pieces(
        height_count, lambda at: second_ref.at[at, 0:128, :], lambda at: q_in.at[at], sems, 4
    )
    copies += kept(lambda at: first_ref.at[at, 192:256, :], chip, core, 0)
    copies += kept(lambda at: chip_ref.at[at], 1 - chip, core, 1)
    copies += kept(lambda at: core_first_ref.at[at, 192:256, :], chip, 1 - core, 2)
    copies += kept(lambda at: core_chip_ref.at[at], 1 - chip, 1 - core, 3)
    for copy in copies:
        copy.start()
    info_copy = pltpu.make_async_copy(info_ref, info_in, info_sem)
    info_copy.start()
    set_margins(kv_ref)
    info_copy.wait()
    listed = info_in[:, 0:2, :].astype(jnp.float32).reshape(2 * height_count, HEAD_DIM)
    source = lax.broadcasted_iota(jnp.int32, listed.shape, 0)
    set_constants(listed, lax.axis_index("tm"), source // 2, bias_ref, height_count)
    for copy in copies:
        copy.wait()

    def q_at(first, count):
        return q_in[pl.ds(first // 2, count // 2)].reshape(count * 64, HEAD_DIM)

    attend(q_at, lambda: None, kv_ref, bias_ref, out_ref, out_in, out_sems, scores)


def side_by_side(refs, rows):
    return jnp.concatenate([jnp.concatenate([refs[i] for i in row], axis=1) for row in rows], axis=0)


def project_large(back_ref, weight_ref, part_ref, weights, sems):
    groups = back_ref.shape[0] // 4

    def copies(g):
        return [
            pltpu.make_async_copy(weight_ref.at[g, 2 * chip], weights.at[chip, g], sems.at[chip, g])
            for chip in range(2)
        ]

    for g in range(groups):
        for copy in copies(g):
            copy.start()
    total = None
    for g in range(0, groups, 2):
        for copy in copies(g) + copies(g + 1):
            copy.wait()
        for chip in range(2):
            first = chip * 2 * groups + g
            rows = [[first + core * groups + i for i in range(2)] for core in range(2)]
            part = jnp.dot(
                side_by_side(back_ref, rows),
                weights[chip, g : g + 2].reshape(2 * HEAD_DIM, weights.shape[-1]),
                preferred_element_type=jnp.float32,
            )
            total = part if total is None else total + part
    part_ref[...] = total


def project_small(
    back_ref, weight_ref, part_ref, out_ref, weights, back_in, out_in, sems, out_sems, back_sem
):
    groups = back_ref.shape[0]
    tiles = sems.shape[0]
    tile = weights.shape[-1]

    def copy_in(n):
        lanes = slice(n * tile, (n + 1) * tile)
        return pltpu.make_async_copy(weight_ref.at[:, 1, :, lanes], weights.at[n], sems.at[n])

    back_copy = pltpu.make_async_copy(back_ref, back_in, back_sem)
    back_copy.start()
    for n in range(tiles):
        copy_in(n).start()
    back_copy.wait()
    attended = side_by_side(back_in, [range(groups)])
    copies_out = []
    for n in range(tiles):
        copy_in(n).wait()
        lanes = slice(n * tile, (n + 1) * tile)
        total = part_ref[:, lanes] + jnp.dot(
            attended,
            weights[n].reshape(groups * HEAD_DIM, tile),
            preferred_element_type=jnp.float32,
        )
        out_in[:, lanes] = total.astype(out_ref.dtype)
        copy = pltpu.make_async_copy(out_in.at[:, lanes], out_ref.at[:, lanes], out_sems.at[n])
        copy.start()
        copies_out.append(copy)
    for copy in copies_out:
        copy.wait()


def by_heads(queries, keys_values, far_cubes, out_weight):
    tm_count = lax.axis_size("tm")
    height_count = lax.axis_size("height")
    devices = tm_count * height_count
    width = queries.shape[-1]
    heads = width // HEAD_DIM
    far_count = far_cubes.shape[-1]
    axes = ("tm", "height")
    bf16, f32 = jnp.bfloat16, jnp.float32
    params = pltpu.CompilerParams(vmem_limit_bytes=36 * 2**20)
    alone = pltpu.CompilerParams(vmem_limit_bytes=60 * 2**20)
    anywhere = pl.BlockSpec(memory_space=pltpu.HBM)
    queries_in = queries.reshape(2, 64, width)
    fields_in = keys_values.reshape(2, 2, 64, width)

    far_lists = far_cubes.reshape(2, heads, far_count).transpose(0, 2, 1)

    first = pl.pallas_call(
        prepare_first,
        in_specs=[anywhere, anywhere, anywhere],
        out_specs=anywhere,
        out_shape=jax.ShapeDtypeStruct((2, 2, height_count, 264, HEAD_DIM), bf16),
        scratch_shapes=[
            pltpu.VMEM((2, 64, width), bf16),
            pltpu.VMEM((2, 2, 64, width), bf16),
            pltpu.VMEM((2, far_count, heads), jnp.int32),
            pltpu.VMEM((2, 2, height_count, 264, HEAD_DIM), bf16),
            pltpu.SemaphoreType.DMA((2, 5)),
            pltpu.SemaphoreType.DMA,
        ],
        compiler_params=alone,
        name="prepare_first",
    )(queries_in, fields_in, far_lists)
    second = pl.pallas_call(
        prepare_second,
        in_specs=[anywhere, pl.BlockSpec(memory_space=pltpu.VMEM)],
        out_specs=anywhere,
        out_shape=jax.ShapeDtypeStruct((height_count, 136, HEAD_DIM), bf16),
        scratch_shapes=[
            pltpu.VMEM((height_count, 2, 64, HEAD_DIM), bf16),
            pltpu.VMEM((height_count, 136, HEAD_DIM), bf16),
            pltpu.SemaphoreType.DMA((height_count,)),
            pltpu.SemaphoreType.DMA,
        ],
        compiler_params=alone,
        cost_estimate=pl.CostEstimate(flops=0, bytes_accessed=2**21, transcendentals=0),
        name="prepare_second",
    )(queries_in, far_lists)

    def exchange(x, over=axes):
        return lax.all_to_all(x, over, 0, 0, tiled=True)

    def swap(x, distance):
        return lax.ppermute(x, "tm", [(i, i ^ distance) for i in range(tm_count)])

    def attention(kernel, name, cubes, shape, operands):
        keys = devices * 128
        work = cubes * 64 * keys
        return pl.pallas_call(
            functools.partial(kernel, height_count),
            in_specs=[anywhere] * operands,
            out_specs=anywhere,
            out_shape=jax.ShapeDtypeStruct(shape, bf16),
            scratch_shapes=[
                pltpu.VMEM((2, devices, 2, 64, 2 * HEAD_DIM), bf16),
                pltpu.VMEM(shape, bf16),
                pltpu.VMEM((shape[0], 8, HEAD_DIM), bf16),
                pltpu.VMEM(shape, bf16),
                pltpu.VMEM((cubes, HEAD_DIM), f32),
                pltpu.SemaphoreType.DMA((5, 4)),
                pltpu.SemaphoreType.DMA((cubes * 64 // ROWS,)),
                pltpu.SemaphoreType.DMA,
                pltpu.VMEM((ROWS, keys), f32),
                pltpu.VMEM((ROWS, keys), f32),
            ],
            compiler_params=params,
            cost_estimate=pl.CostEstimate(
                flops=8 * work * HEAD_DIM, bytes_accessed=4 * 2**20, transcendentals=work
            ),
            name=name,
        )

    vmem = pl.BlockSpec(memory_space=pltpu.VMEM)
    got_first = exchange(first.reshape(devices, 264, HEAD_DIM))
    got_first, second = lax.optimization_barrier((got_first, second))
    small = got_first[:, 192:256]
    info = got_first[:, 256:264]
    second, small = lax.optimization_barrier((second, small))
    got_second = exchange(second, "height")
    core_first = swap(got_first, 1)
    chip = swap(small, 2)
    out_large = attention(large_kernel, "attend_large", devices, (devices, 64, HEAD_DIM), 3)(
        got_first, core_first, info
    )
    core_chip = swap(chip, 1)

    got_second, out_large = lax.optimization_barrier((got_second, out_large))
    back_large = exchange(out_large)
    out_small = attention(small_kernel, "attend_small", 2 * height_count, (height_count, 128, HEAD_DIM), 6)(
        got_first, got_second, chip, core_first, core_chip, got_second[:, 128:136]
    )
    back_large, out_small = lax.optimization_barrier((back_large, out_small))
    back_small = exchange(out_small, "height")
    by_head = out_weight.reshape(height_count, 3, HEAD_DIM, width)
    part = pl.pallas_call(
        project_large,
        in_specs=[vmem, anywhere],
        out_shape=pltpu.VMEM((128, width), f32),
        scratch_shapes=[
            pltpu.VMEM((2, height_count, HEAD_DIM, width), bf16),
            pltpu.SemaphoreType.DMA((2, height_count)),
        ],
        compiler_params=pltpu.CompilerParams(vmem_limit_bytes=50 * 2**20),
        cost_estimate=pl.CostEstimate(
            flops=4 * 128 * width * width // 3, bytes_accessed=14 * 2**20, transcendentals=0
        ),
        name="project_large",
    )(back_large, by_head)
    back_small, part = lax.optimization_barrier((back_small, part))
    output = pl.pallas_call(
        project_small,
        in_specs=[anywhere, anywhere, vmem],
        out_specs=anywhere,
        out_shape=jax.ShapeDtypeStruct((128, width), bf16),
        scratch_shapes=[
            pltpu.VMEM((6, height_count, HEAD_DIM, width // 6), bf16),
            pltpu.VMEM(back_small.shape, bf16),
            pltpu.VMEM((128, width), bf16),
            pltpu.SemaphoreType.DMA((6,)),
            pltpu.SemaphoreType.DMA((6,)),
            pltpu.SemaphoreType.DMA,
        ],
        compiler_params=pltpu.CompilerParams(vmem_limit_bytes=50 * 2**20),
        cost_estimate=pl.CostEstimate(
            flops=2 * 128 * width * width // 3, bytes_accessed=8 * 2**20, transcendentals=0
        ),
        name="project_small",
    )(back_small, by_head, part)
    return output.reshape(queries.shape)


def solution(mesh):
    in_specs = (
        P("tm", "height", None, None, None),
        P("tm", "height", None, None, None, None),
        P("tm", "height", None, None, None),
        P(),
    )
    out_specs = P("tm", "height", None, None, None)
    fits = mesh.shape["tm"] == 4 and HEADS == 3 * mesh.shape["height"]
    return jax.shard_map(by_heads if fits else body, mesh=mesh, in_specs=in_specs, out_specs=out_specs, check_vma=False)
```

```python
import functools
import math

import jax
import jax.numpy as jnp
import ml_dtypes
import numpy as np
from jax import lax
from jax.experimental import pallas as pl
from jax.experimental.pallas import tpu as pltpu
from jax.sharding import PartitionSpec as P

HEADS = 24
SLOTS = 512
HEAD_DIM = 128
LOG2E = math.log2(math.e)
SCALE = LOG2E / math.sqrt(HEAD_DIM)
TWICE = 1.0 / SCALE
TWICE_HIGH = float(np.asarray(TWICE, ml_dtypes.bfloat16))
TWICE_LOW = TWICE - TWICE_HIGH
ROWS = 512
CHUNK = 512


def padded_2(shard, sides, width):
    for axis, dim in sides:
        peers, length = (lax.axis_size(axis), shard.shape[dim])
        up = [(i, (i + 1) % peers) for i in range(peers - 1)]
        down = [(j, i) for i, j in up]
        last = lax.slice_in_dim(shard, length - width, length, axis=dim)
        leading = lax.slice_in_dim(shard, 0, width, axis=dim)
        before = lax.ppermute(last, axis, up)
        after = lax.ppermute(leading, axis, down)
        shard = jnp.concatenate([before, shard, after], axis=dim)
    return shard


def body(queries, keys_values, far_cubes, out_weight):
    tm_count = lax.axis_size("tm")
    height_count = lax.axis_size("height")
    device_count = tm_count * height_count
    capacity = SLOTS // device_count
    span_time, span_height, span_width, cube, width = queries.shape
    heads = HEADS
    head_size = width // heads
    far_count = far_cubes.shape[-1]
    local_count = span_time * span_height * span_width
    grid_time = span_time * tm_count
    grid_height = span_height * height_count
    far_ids = far_cubes.reshape(local_count, heads, far_count)
    far_time = far_ids // (grid_height * span_width)
    far_height = far_ids // span_width % grid_height
    far_width = far_ids % span_width
    owner_dev = far_time // span_time * height_count + far_height // span_height
    local_cube = (
        far_time % span_time * span_height + far_height % span_height
    ) * span_width + far_width
    tile_code = local_cube * heads + jnp.arange(heads, dtype=jnp.int32)[None, :, None]
    wanted = (
        jnp.zeros((device_count, local_count * heads), jnp.int32).at[owner_dev, tile_code].max(1)
    )
    slot_rank = jnp.cumsum(wanted, axis=1) - 1
    far_slot = owner_dev * capacity + slot_rank[owner_dev, tile_code]
    target = jnp.where(wanted > 0, slot_rank, capacity)
    columns = jnp.broadcast_to(
        jnp.arange(local_count * heads, dtype=jnp.int32)[None, :], wanted.shape
    )
    rows = jnp.broadcast_to(jnp.arange(device_count, dtype=jnp.int32)[:, None], wanted.shape)
    requests = (
        jnp.zeros((device_count, capacity + 1), jnp.int32)
        .at[rows, target]
        .set(columns)[:, :capacity]
    )
    source = keys_values.reshape(local_count, 2, cube, heads, head_size)
    padded = padded_2(keys_values, (("tm", 0), ("height", 1)), 1)
    padded = jnp.pad(padded, ((0, 0), (0, 0), (1, 1), (0, 0), (0, 0), (0, 0)))
    asked = lax.all_to_all(requests, ("tm", "height"), split_axis=0, concat_axis=0, tiled=True)
    tiles = lax.all_to_all(
        source[asked // heads, :, :, asked % heads, :],
        ("tm", "height"),
        split_axis=0,
        concat_axis=0,
        tiled=True,
    )
    received = tiles.reshape(device_count * capacity, 2, cube, head_size)
    first_time = lax.axis_index("tm") * span_time
    first_height = lax.axis_index("height") * span_height
    offsets = jnp.arange(3, dtype=jnp.int32) - 1
    scale = 1.0 / math.sqrt(head_size)
    zero = jnp.zeros((), jnp.int32)
    flat_queries = queries.reshape(local_count, cube, heads, head_size)

    def one_cube(index):
        time_pos = index // (span_height * span_width)
        height_pos = index // span_width % span_height
        width_pos = index % span_width
        window = lax.dynamic_slice(
            padded, (time_pos, height_pos, width_pos, zero, zero, zero), (3, 3, 3, 2, cube, width)
        )
        window = window.reshape(27, 2, cube, heads, head_size)
        global_time = first_time + time_pos + offsets
        global_height = first_height + height_pos + offsets
        global_width = width_pos + offsets
        inside_time = (global_time >= 0) & (global_time < grid_time)
        inside_height = (global_height >= 0) & (global_height < grid_height)
        inside_width = (global_width >= 0) & (global_width < span_width)
        valid = (
            inside_time[:, None, None] & inside_height[None, :, None] & inside_width[None, None, :]
        ).reshape(27)
        keys_window = window[:, 0].reshape(27 * cube, heads, head_size)
        values_window = window[:, 1].reshape(27 * cube, heads, head_size)
        far_tiles = received[far_slot[index]]
        query = flat_queries[index]
        score_window = (
            jnp.einsum("qhd,khd->hqk", query, keys_window, preferred_element_type=jnp.float32)
            * scale
        )
        score_window = jnp.where(jnp.repeat(valid, cube)[None, None, :], score_window, -jnp.inf)
        score_far = (
            jnp.einsum(
                "qhd,hfkd->hqfk", query, far_tiles[:, :, 0], preferred_element_type=jnp.float32
            )
            * scale
        )
        scores = jnp.concatenate(
            [score_window, score_far.reshape(heads, cube, far_count * cube)], axis=-1
        )
        largest = jnp.max(scores, axis=-1, keepdims=True)
        lifted = jnp.exp(scores - largest)
        weights = (lifted / jnp.sum(lifted, axis=-1, keepdims=True)).astype(jnp.bfloat16)
        attended = jnp.einsum(
            "hqk,khd->qhd",
            weights[:, :, : 27 * cube],
            values_window,
            preferred_element_type=jnp.float32,
        )
        far_weights = weights[:, :, 27 * cube :].reshape(heads, cube, far_count, cube)
        attended = attended + jnp.einsum(
            "hqfk,hfkd->qhd", far_weights, far_tiles[:, :, 1], preferred_element_type=jnp.float32
        )
        return attended.reshape(cube, width).astype(jnp.bfloat16)

    attended = lax.map(one_cube, jnp.arange(local_count, dtype=jnp.int32))
    output = jnp.dot(
        attended.reshape(local_count * cube, width), out_weight, preferred_element_type=jnp.float32
    )
    return output.astype(jnp.bfloat16).reshape(queries.shape)


def head_lanes(head):
    return slice(head * HEAD_DIM, (head + 1) * HEAD_DIM)


def list_counts(far_ref, w, head):
    cubes = lax.broadcasted_iota(jnp.int32, (far_ref.shape[1], HEAD_DIM), 1) % 64
    listed = (far_ref[w, :, head : head + 1] == cubes).astype(jnp.float32)
    return jnp.sum(listed, axis=0, keepdims=True).astype(jnp.bfloat16)


def prepare_first(q_ref, kv_ref, far_ref, out_ref, q_in, kv_in, far_in, staged, sems, far_sem):
    groups = out_ref.shape[2]

    def copies_in(core):
        return [
            pltpu.make_async_copy(q_ref.at[core], q_in.at[core], sems.at[core, 0]),
            pltpu.make_async_copy(kv_ref.at[core, 0], kv_in.at[core, 0], sems.at[core, 1]),
            pltpu.make_async_copy(kv_ref.at[core, 1], kv_in.at[core, 1], sems.at[core, 2]),
        ]

    def copy_out(chip, core):
        return pltpu.make_async_copy(
            staged.at[chip, core], out_ref.at[chip, core], sems.at[core, 3 + chip]
        )

    far_copy = pltpu.make_async_copy(far_ref, far_in, far_sem)
    far_copy.start()
    for core in range(2):
        for copy in copies_in(core):
            copy.start()
    far_copy.wait()
    for core in range(2):
        for chip in range(2):
            for g in range(groups):
                counts = list_counts(far_in, core, 3 * g + 2 * chip)
                staged[chip, core, g, 256:264, :] = jnp.broadcast_to(counts, (8, HEAD_DIM))
        for copy in copies_in(core):
            copy.wait()
        for chip in range(2):
            for g in range(groups):
                lanes = head_lanes(3 * g + 2 * chip)
                staged[chip, core, g, 0:64, :] = q_in[core, :, lanes]
                staged[chip, core, g, 64:128, :] = kv_in[core, 0, :, lanes]
                staged[chip, core, g, 128:192, :] = kv_in[core, 1, :, lanes]
                staged[chip, core, g, 192:256, :] = kv_in[core, chip, :, head_lanes(3 * g + 1)]
            copy_out(chip, core).start()
    for core in range(2):
        for chip in range(2):
            copy_out(chip, core).wait()


def prepare_second(q_ref, far_ref, out_ref, q_in, staged, sems, out_sem):
    groups = out_ref.shape[0]
    copies = [
        pltpu.make_async_copy(
            q_ref.at[:, :, pl.ds((3 * g + 1) * HEAD_DIM, HEAD_DIM)], q_in.at[g], sems.at[g]
        )
        for g in range(groups)
    ]
    for copy in copies:
        copy.start()
    top_row = lax.broadcasted_iota(jnp.int32, (8, HEAD_DIM), 0) == 0
    for g in range(groups):
        counts = [list_counts(far_ref, w, 3 * g + 1).astype(jnp.float32) for w in range(2)]
        staged[g, 128:136, :] = jnp.where(top_row, *counts).astype(jnp.bfloat16)
        copies[g].wait()
        staged[g, 0:64, :] = q_in[g, 0]
        staged[g, 64:128, :] = q_in[g, 1]
    copy = pltpu.make_async_copy(staged, out_ref, out_sem)
    copy.start()
    copy.wait()


def set_constants(listed, time, height, bias_ref, height_count):
    lane = lax.broadcasted_iota(jnp.int32, listed.shape, 1)
    place = lane % 64 // 2
    near = (jnp.abs(time - place // height_count) <= 1) & (
        jnp.abs(height - place % height_count) <= 1
    )
    counts = listed + jnp.where(near, 1.0, 0.0)
    high = lane < 64
    bias_ref[...] = jnp.where(
        counts < 0.5,
        jnp.where(high, -1e30, 0.0),
        jnp.where(counts > 1.5, jnp.where(high, TWICE_HIGH, TWICE_LOW), 0.0),
    )


def set_margins(kv_ref):
    shape = (2, 64, HEAD_DIM)
    width = lax.broadcasted_iota(jnp.int32, shape, 0)
    lane = lax.broadcasted_iota(jnp.int32, shape, 2) % 64
    for s in range(kv_ref.shape[1]):
        kv_ref[0, s, :, :, HEAD_DIM:] = (lane == 2 * s + width).astype(jnp.bfloat16)
        kv_ref[1, s, :, :, HEAD_DIM:] = jnp.ones(shape, jnp.bfloat16)


def attend(q_at, wait_values, kv_ref, bias_ref, out_ref, out_in, out_sems, scores):
    sources, tokens = bias_ref.shape[0], 64
    step = ROWS // tokens
    chunk = CHUNK // 128
    chunks = range(0, kv_ref.shape[1], chunk)
    fold = out_ref.shape[1] // tokens

    def copy_out(first):
        at = pl.ds(first // fold, step // fold)
        return pltpu.make_async_copy(out_in.at[at], out_ref.at[at], out_sems.at[first // step])

    def score(first, s_ref):
        bias = [
            jnp.broadcast_to(bias_ref[pl.ds(first + i, 1), :], (tokens, HEAD_DIM))
            for i in range(step)
        ]
        bias = jnp.concatenate(bias, axis=0).astype(jnp.bfloat16)
        query = jnp.concatenate([q_at(first, step), bias], axis=1)
        top = None
        for s in chunks:
            part = lax.dot_general(
                query,
                kv_ref[0, s : s + chunk].reshape(CHUNK, 2 * HEAD_DIM),
                (((1,), (1,)), ((), ())),
                preferred_element_type=jnp.float32,
            )
            s_ref[:, s * 128 : s * 128 + CHUNK] = part
            for lane in range(0, CHUNK, HEAD_DIM):
                piece = part[:, lane : lane + HEAD_DIM]
                top = piece if top is None else jnp.maximum(top, piece)
        return jnp.max(top, axis=1, keepdims=True)

    def mix(first, s_ref, largest):
        mixed = jnp.zeros((ROWS, 2 * HEAD_DIM), jnp.float32)
        for s in chunks:
            lifted = jnp.exp2((s_ref[:, s * 128 : s * 128 + CHUNK] - largest) * SCALE)
            mixed += jnp.dot(
                lifted.astype(jnp.bfloat16),
                kv_ref[1, s : s + chunk].reshape(CHUNK, 2 * HEAD_DIM),
                preferred_element_type=jnp.float32,
            )
        result = (mixed[:, :HEAD_DIM] / mixed[:, HEAD_DIM:]).astype(out_ref.dtype)
        at = pl.ds(first // fold, step // fold)
        out_in[at] = result.reshape(step // fold, fold * tokens, HEAD_DIM)
        copy_out(first).start()

    def two_blocks(index, largest):
        first = index * 2 * step
        later = score(first + step, scores[1])
        mix(first, scores[0], largest)
        largest = score(first + 2 * step, scores[0])
        mix(first + step, scores[1], later)
        return largest

    largest = score(0, scores[0])
    wait_values()
    largest = lax.fori_loop(0, sources // step // 2 - 1, two_blocks, largest)
    last = sources - step
    later = score(last, scores[1])
    mix(last - step, scores[0], largest)
    mix(last, scores[1], later)
    for first in range(0, sources, step):
        copy_out(first).wait()


def pieces(count, source, target, sems, row):
    part = count // 2
    return [
        pltpu.make_async_copy(
            source(pl.ds(i * part, part)), target(pl.ds(i * part, part)), sems.at[row, i]
        )
        for i in range(2)
    ]


def large_kernel(
    height_count, mine_ref, core_ref, info_ref, out_ref, kv_ref, q_in, info_in, out_in, bias_ref,
    sems, out_sems, info_sem, *scores
):
    core = lax.axis_index("tm") % 2
    count = mine_ref.shape[0]
    own = [
        pieces(
            count,
            lambda at, k=k: mine_ref.at[at, 64 + 64 * k : 128 + 64 * k, :],
            lambda at, k=k: kv_ref.at[k, at, core, :, 0:HEAD_DIM],
            sems,
            k,
        )
        for k in range(2)
    ]
    other = [
        pieces(
            count,
            lambda at, k=k: core_ref.at[at, 64 + 64 * k : 128 + 64 * k, :],
            lambda at, k=k: kv_ref.at[k, at, 1 - core, :, 0:HEAD_DIM],
            sems,
            2 + k,
        )
        for k in range(2)
    ]
    query = pieces(count, lambda at: mine_ref.at[at, 0:64, :], lambda at: q_in.at[at], sems, 4)
    for copy in own[0] + other[0] + query + own[1] + other[1]:
        copy.start()
    info_copy = pltpu.make_async_copy(info_ref, info_in, info_sem)
    info_copy.start()
    set_margins(kv_ref)
    info_copy.wait()
    listed = info_in[:, 0, :].astype(jnp.float32)
    source = lax.broadcasted_iota(jnp.int32, listed.shape, 0)
    set_constants(listed, source // height_count, source % height_count, bias_ref, height_count)
    for copy in own[0] + other[0] + query:
        copy.wait()

    def wait_values():
        for copy in own[1] + other[1]:
            copy.wait()

    def q_at(first, count):
        return q_in[pl.ds(first, count)].reshape(count * 64, HEAD_DIM)

    attend(q_at, wait_values, kv_ref, bias_ref, out_ref, out_in, out_sems, scores)


def small_kernel(
    height_count, first_ref, second_ref, chip_ref, core_first_ref, core_chip_ref, info_ref, out_ref,
    kv_ref, q_in, info_in, out_in, bias_ref, sems, out_sems, info_sem, *scores
):
    core = lax.axis_index("tm") % 2
    chip = lax.axis_index("tm") // 2
    count = first_ref.shape[0]

    def kept(source, kind, width, row):
        return pieces(
            count, source, lambda at: kv_ref.at[kind, at, width, :, 0:HEAD_DIM], sems, row
        )

    copies = pieces(
        height_count, lambda at: second_ref.at[at, 0:128, :], lambda at: q_in.at[at], sems, 4
    )
    copies += kept(lambda at: first_ref.at[at, 192:256, :], chip, core, 0)
    copies += kept(lambda at: chip_ref.at[at], 1 - chip, core, 1)
    copies += kept(lambda at: core_first_ref.at[at, 192:256, :], chip, 1 - core, 2)
    copies += kept(lambda at: core_chip_ref.at[at], 1 - chip, 1 - core, 3)
    for copy in copies:
        copy.start()
    info_copy = pltpu.make_async_copy(info_ref, info_in, info_sem)
    info_copy.start()
    set_margins(kv_ref)
    info_copy.wait()
    listed = info_in[:, 0:2, :].astype(jnp.float32).reshape(2 * height_count, HEAD_DIM)
    source = lax.broadcasted_iota(jnp.int32, listed.shape, 0)
    set_constants(listed, lax.axis_index("tm"), source // 2, bias_ref, height_count)
    for copy in copies:
        copy.wait()

    def q_at(first, count):
        return q_in[pl.ds(first // 2, count // 2)].reshape(count * 64, HEAD_DIM)

    attend(q_at, lambda: None, kv_ref, bias_ref, out_ref, out_in, out_sems, scores)


def side_by_side(refs, rows):
    return jnp.concatenate([jnp.concatenate([refs[i] for i in row], axis=1) for row in rows], axis=0)


def project_large(back_ref, weight_ref, part_ref, weights, sems):
    groups = back_ref.shape[0] // 4

    def copies(g):
        return [
            pltpu.make_async_copy(weight_ref.at[g, 2 * chip], weights.at[chip, g], sems.at[chip, g])
            for chip in range(2)
        ]

    for g in range(groups):
        for copy in copies(g):
            copy.start()
    total = None
    for g in range(0, groups, 2):
        for copy in copies(g) + copies(g + 1):
            copy.wait()
        for chip in range(2):
            first = chip * 2 * groups + g
            rows = [[first + core * groups + i for i in range(2)] for core in range(2)]
            part = jnp.dot(
                side_by_side(back_ref, rows),
                weights[chip, g : g + 2].reshape(2 * HEAD_DIM, weights.shape[-1]),
                preferred_element_type=jnp.float32,
            )
            total = part if total is None else total + part
    part_ref[...] = total


def project_small(
    back_ref, weight_ref, part_ref, out_ref, weights, back_in, out_in, sems, out_sems, back_sem
):
    groups = back_ref.shape[0]
    tiles = sems.shape[0]
    tile = weights.shape[-1]

    def copy_in(n):
        lanes = slice(n * tile, (n + 1) * tile)
        return pltpu.make_async_copy(weight_ref.at[:, 1, :, lanes], weights.at[n], sems.at[n])

    back_copy = pltpu.make_async_copy(back_ref, back_in, back_sem)
    back_copy.start()
    for n in range(tiles):
        copy_in(n).start()
    back_copy.wait()
    attended = side_by_side(back_in, [range(groups)])
    copies_out = []
    for n in range(tiles):
        copy_in(n).wait()
        lanes = slice(n * tile, (n + 1) * tile)
        total = part_ref[:, lanes] + jnp.dot(
            attended,
            weights[n].reshape(groups * HEAD_DIM, tile),
            preferred_element_type=jnp.float32,
        )
        out_in[:, lanes] = total.astype(out_ref.dtype)
        copy = pltpu.make_async_copy(out_in.at[:, lanes], out_ref.at[:, lanes], out_sems.at[n])
        copy.start()
        copies_out.append(copy)
    for copy in copies_out:
        copy.wait()


def by_heads(queries, keys_values, far_cubes, out_weight):
    tm_count = lax.axis_size("tm")
    height_count = lax.axis_size("height")
    devices = tm_count * height_count
    width = queries.shape[-1]
    heads = width // HEAD_DIM
    far_count = far_cubes.shape[-1]
    axes = ("tm", "height")
    bf16, f32 = jnp.bfloat16, jnp.float32
    params = pltpu.CompilerParams(vmem_limit_bytes=36 * 2**20)
    alone = pltpu.CompilerParams(vmem_limit_bytes=60 * 2**20)
    anywhere = pl.BlockSpec(memory_space=pltpu.HBM)
    queries_in = queries.reshape(2, 64, width)
    fields_in = keys_values.reshape(2, 2, 64, width)

    far_lists = far_cubes.reshape(2, heads, far_count).transpose(0, 2, 1)

    first = pl.pallas_call(
        prepare_first,
        in_specs=[anywhere, anywhere, anywhere],
        out_specs=anywhere,
        out_shape=jax.ShapeDtypeStruct((2, 2, height_count, 264, HEAD_DIM), bf16),
        scratch_shapes=[
            pltpu.VMEM((2, 64, width), bf16),
            pltpu.VMEM((2, 2, 64, width), bf16),
            pltpu.VMEM((2, far_count, heads), jnp.int32),
            pltpu.VMEM((2, 2, height_count, 264, HEAD_DIM), bf16),
            pltpu.SemaphoreType.DMA((2, 5)),
            pltpu.SemaphoreType.DMA,
        ],
        compiler_params=alone,
        name="prepare_first",
    )(queries_in, fields_in, far_lists)
    second = pl.pallas_call(
        prepare_second,
        in_specs=[anywhere, pl.BlockSpec(memory_space=pltpu.VMEM)],
        out_specs=anywhere,
        out_shape=jax.ShapeDtypeStruct((height_count, 136, HEAD_DIM), bf16),
        scratch_shapes=[
            pltpu.VMEM((height_count, 2, 64, HEAD_DIM), bf16),
            pltpu.VMEM((height_count, 136, HEAD_DIM), bf16),
            pltpu.SemaphoreType.DMA((height_count,)),
            pltpu.SemaphoreType.DMA,
        ],
        compiler_params=alone,
        cost_estimate=pl.CostEstimate(flops=0, bytes_accessed=2**21, transcendentals=0),
        name="prepare_second",
    )(queries_in, far_lists)

    def exchange(x, over=axes):
        return lax.all_to_all(x, over, 0, 0, tiled=True)

    def swap(x, distance):
        return lax.ppermute(x, "tm", [(i, i ^ distance) for i in range(tm_count)])

    def attention(kernel, name, cubes, shape, operands):
        keys = devices * 128
        work = cubes * 64 * keys
        return pl.pallas_call(
            functools.partial(kernel, height_count),
            in_specs=[anywhere] * operands,
            out_specs=anywhere,
            out_shape=jax.ShapeDtypeStruct(shape, bf16),
            scratch_shapes=[
                pltpu.VMEM((2, devices, 2, 64, 2 * HEAD_DIM), bf16),
                pltpu.VMEM(shape, bf16),
                pltpu.VMEM((shape[0], 8, HEAD_DIM), bf16),
                pltpu.VMEM(shape, bf16),
                pltpu.VMEM((cubes, HEAD_DIM), f32),
                pltpu.SemaphoreType.DMA((5, 4)),
                pltpu.SemaphoreType.DMA((cubes * 64 // ROWS,)),
                pltpu.SemaphoreType.DMA,
                pltpu.VMEM((ROWS, keys), f32),
                pltpu.VMEM((ROWS, keys), f32),
            ],
            compiler_params=params,
            cost_estimate=pl.CostEstimate(
                flops=8 * work * HEAD_DIM, bytes_accessed=4 * 2**20, transcendentals=work
            ),
            name=name,
        )

    vmem = pl.BlockSpec(memory_space=pltpu.VMEM)
    got_first = exchange(first.reshape(devices, 264, HEAD_DIM))
    got_first, second = lax.optimization_barrier((got_first, second))
    small = got_first[:, 192:256]
    info = got_first[:, 256:264]
    second, small = lax.optimization_barrier((second, small))
    got_second = exchange(second, "height")
    core_first = swap(got_first, 1)
    chip = swap(small, 2)
    out_large = attention(large_kernel, "attend_large", devices, (devices, 64, HEAD_DIM), 3)(
        got_first, core_first, info
    )
    core_chip = swap(chip, 1)

    got_second, out_large = lax.optimization_barrier((got_second, out_large))
    back_large = exchange(out_large)
    out_small = attention(small_kernel, "attend_small", 2 * height_count, (height_count, 128, HEAD_DIM), 6)(
        got_first, got_second, chip, core_first, core_chip, got_second[:, 128:136]
    )
    back_large, out_small = lax.optimization_barrier((back_large, out_small))
    back_small = exchange(out_small, "height")
    by_head = out_weight.reshape(height_count, 3, HEAD_DIM, width)
    part = pl.pallas_call(
        project_large,
        in_specs=[vmem, anywhere],
        out_shape=pltpu.VMEM((128, width), f32),
        scratch_shapes=[
            pltpu.VMEM((2, height_count, HEAD_DIM, width), bf16),
            pltpu.SemaphoreType.DMA((2, height_count)),
        ],
        compiler_params=pltpu.CompilerParams(vmem_limit_bytes=50 * 2**20),
        cost_estimate=pl.CostEstimate(
            flops=4 * 128 * width * width // 3, bytes_accessed=14 * 2**20, transcendentals=0
        ),
        name="project_large",
    )(back_large, by_head)
    back_small, part = lax.optimization_barrier((back_small, part))
    output = pl.pallas_call(
        project_small,
        in_specs=[anywhere, anywhere, vmem],
        out_specs=anywhere,
        out_shape=jax.ShapeDtypeStruct((128, width), bf16),
        scratch_shapes=[
            pltpu.VMEM((6, height_count, HEAD_DIM, width // 6), bf16),
            pltpu.VMEM(back_small.shape, bf16),
            pltpu.VMEM((128, width), bf16),
            pltpu.SemaphoreType.DMA((6,)),
            pltpu.SemaphoreType.DMA((6,)),
            pltpu.SemaphoreType.DMA,
        ],
        compiler_params=pltpu.CompilerParams(vmem_limit_bytes=50 * 2**20),
        cost_estimate=pl.CostEstimate(
            flops=2 * 128 * width * width // 3, bytes_accessed=8 * 2**20, transcendentals=0
        ),
        name="project_small",
    )(back_small, by_head, part)
    return output.reshape(queries.shape)


def solution(mesh):
    in_specs = (
        P("tm", "height", None, None, None),
        P("tm", "height", None, None, None, None),
        P("tm", "height", None, None, None),
        P(),
    )
    out_specs = P("tm", "height", None, None, None)
    fits = mesh.shape["tm"] == 4 and HEADS == 3 * mesh.shape["height"]
    return jax.shard_map(by_heads if fits else body, mesh=mesh, in_specs=in_specs, out_specs=out_specs, check_vma=False)
```
